128 devices in a mesh: outer: 2 (over core), ep: 16 (over z, x), tp: 4 (over y).
Axes of the slice: x: 4, y: 4, z: 4, core: 2. Of those that a mesh axis runs over, the one named last changes fastest.
Arguments:
- tokens: bfloat16 [4096, 3584], P(('outer', 'ep')), may hold values from -27 to 27
- norm_gain: float32 [3584], replicated, may hold values from 0.5 to 1.5
- dense_weight: bfloat16 [3, 3584, 2560], P(None, 'outer', 'tp'), may hold values from -0.09375 to 0.09375
- expert_gate_up: bfloat16 [16, 2, 3584, 2560], P('ep', None, None, 'tp'), may hold values from -0.09375 to 0.09375
- expert_down: bfloat16 [16, 3584, 2560], P('ep', None, 'tp'), may hold values from -0.125 to 0.125
- expert_ids: int32 [4096, 2], P(('outer', 'ep')), may hold values from 0 to 15, all different within a row; in each aligned block of 128 rows (0 to 127, 128 to 255, ...) at most 24 rows name the same one
- gate_weights: float32 [4096, 2], P(('outer', 'ep')), may hold values from 0.1 to 1
- grad_out: bfloat16 [4096, 3584], P(('outer', 'ep')), may hold values from -6 to 6
Outputs:
- layer_out: bfloat16 [4096, 3584], P(('outer', 'ep'))
- grad_in: bfloat16 [4096, 3584], P(('outer', 'ep'))
The draws below stay inside these ranges and needn't reach their ends.
Inputs may be any that keep to these rules, and one draw needn't show every extreme that they name: `expert_ids`: each row names two different experts. Of the 128 rows of one device at most 24 name any one expert, and in every draw some device has exactly 24 rows naming one expert.
All inputs are finite; a program needn't handle non-finite values.
Results may differ from the reference program's by a relative error of at most 0.009.
Values may be sent and summed in bfloat16 or wider, within the bound.
A program may use at most 128 MiB of HBM per device.

```python
import math
import jax
import jax.numpy as jnp
import numpy as np
from jax import lax

D = 3584
HE = 2560
FF = 2560
TOK_DEV = 128
EXPERTS = 16
TOKENS = 4096
MOST = 24
N_OUTER = 2
N_EP = 16
N_TP = 4


def draw_tokens(key, part):
    key = jax.random.fold_in(key, 7)
    subkeys = jax.random.split(key, 4)
    base_values = jnp.clip(jax.random.normal(subkeys[1], (TOKENS, D), jnp.float32), -3.0, 3.0)
    row_low, row_high, col_low, col_high = (0.3, 3.0, 0.3, 3.0)
    row_scale = jnp.exp(jax.random.uniform(subkeys[2], (TOKENS, 1), jnp.float32, minval=math.log(row_low), maxval=math.log(row_high)))
    col_scale = jnp.exp(jax.random.uniform(subkeys[3], (1, D), jnp.float32, minval=math.log(col_low), maxval=math.log(col_high)))
    return (base_values * row_scale * col_scale).astype(jnp.bfloat16)


def level_of(key, shape, cuts, least, high):
    gain, own = 1.0, jax.random.fold_in(key, 6)
    for axis_at, shards_of in cuts:
        heights = jnp.exp(jax.random.uniform(jax.random.fold_in(own, axis_at), (shards_of,), jnp.float32, least / len(cuts), high / len(cuts)))
        gain = gain * jnp.repeat(heights, shape[axis_at] // shards_of).reshape([-1 if axis == axis_at else 1 for axis in range(len(shape))])
    return gain


def deal_out(stream_key, own, number, rows, amount, top, bound, slope):
    sequence = jax.random.permutation(stream_key, amount)
    packed, usual = portions_of(amount, rows * top, bound, slope, True), portions_of(amount, rows * top, bound, slope, False)
    places = jnp.arange(amount)

    def named(tallies, rotation):
        used = int((tallies > 0).sum())
        fixed = max(1, used // 4)
        shifted = fixed + (places - fixed + rotation * (used - fixed)) % max(1, amount - fixed)
        return jnp.zeros((amount,), jnp.int32).at[sequence[jnp.where(places < fixed, places, shifted)]].set(jnp.asarray(tallies, jnp.int32))

    tallies = jnp.where(number % 4 == 0, named(packed, number // 4), named(usual, number - number // 4 - 1))
    mixed = jax.random.permutation(jax.random.fold_in(own, 3), amount)
    source_of, receiver = mixed[0:amount // 2 * 2:2], mixed[1:amount // 2 * 2:2]
    slack = jnp.minimum(tallies[source_of] - 1, bound - tallies[receiver]) // 2
    slack = jnp.where((source_of == sequence[0]) | (receiver == sequence[0]) | (tallies[receiver] == 0), 0, jnp.maximum(slack, 0))
    shifted = jax.random.randint(jax.random.fold_in(own, 4), (amount // 2,), 0, 1 << 20) % (slack + 1)
    tallies = tallies.at[source_of].add(-shifted).at[receiver].add(shifted)
    items = jnp.searchsorted(jnp.cumsum(tallies), jnp.arange(rows * top), side="right").astype(jnp.int32)
    table = items.reshape(top, rows).T
    table = table[jax.random.permutation(jax.random.fold_in(own, 1), rows)]
    rotation = jax.random.randint(jax.random.fold_in(own, 2), (rows, 1), 0, top)
    return jnp.take_along_axis(table, (jnp.arange(top)[None, :] + rotation) % top, axis=1)


def portions_of(count, total, limit, skew, full):
    loads = [(1 << 20) // math.isqrt(grade ** skew) + 1 for grade in range(1, count + 1)]
    largest = limit if full else min(limit, max(-(-total // count), total * loads[0] // sum(loads)))
    least = 1 if total - largest >= count - 1 else 0
    holding, surplus = [largest] + [least] * (count - 1), total - largest - least * (count - 1)
    while surplus > 0:
        candidates = [i for i in range(1, count) if holding[i] < largest] or [i for i in range(1, count) if holding[i] < limit]
        mass, left = sum([loads[i] for i in candidates]), surplus
        for i in candidates:
            extra = min(limit - holding[i], max(1, left * loads[i] // mass), surplus)
            holding[i] = holding[i] + extra
            surplus = surplus - extra
    return np.array(holding)


def noise(rng, extent, scale, limit, cuts=(), kind=jnp.bfloat16):
    gain = level_of(rng, extent, cuts, -0.22, 0.18) if cuts else 1.0
    array = jax.random.normal(rng, extent, jnp.float32) * scale * gain
    return jnp.minimum(jnp.maximum(array, -limit), limit).astype(kind)


def setup_inputs(seed: int = 0) -> dict:
    key_list = jax.random.split(jax.random.key(seed), 9)
    tokens = draw_tokens(jax.random.fold_in(key_list[8], 71), 0)
    norm_gain = jnp.clip(1.0 + 0.1 * jax.random.normal(key_list[1], (D,), jnp.float32), 0.5, 1.5)
    dense_weight = noise(key_list[2], (3, D, FF), D ** -0.5, 0.09375, ((1, 2), (2, 4)))
    expert_gate_up = noise(key_list[3], (EXPERTS, 2, D, HE), D ** -0.5, 0.09375, ((0, 16), (3, 4)))
    expert_down = noise(key_list[4], (EXPERTS, D, HE), HE ** -0.5, 0.125, ((0, 16), (2, 4)))
    expert_ids_keys = jax.random.split(jax.random.fold_in(key_list[5], 1), TOKENS // TOK_DEV)
    expert_ids_turns = jax.random.permutation(jax.random.fold_in(key_list[5], 3), TOKENS // TOK_DEV)
    expert_ids = jax.vmap(lambda own, number: deal_out(jax.random.fold_in(key_list[5], 2), own, number, TOK_DEV, EXPERTS, 2, MOST, 2))(expert_ids_keys, expert_ids_turns).reshape((TOKENS, 2))
    gate_weights = jnp.clip(jnp.exp(math.log(1.0) - 2.3025851 * jax.random.uniform(key_list[6], (TOKENS, 2), jnp.float32) ** level_of(key_list[6], (TOKENS, 2), ((0, 32),), -0.2, 0.2)), 0.1, 1.0)
    grad_out = noise(key_list[7], (TOKENS, D), 1.0, 6.0, ((0, 32),))
    return {"tokens": tokens, "norm_gain": norm_gain, "dense_weight": dense_weight, "expert_gate_up": expert_gate_up, "expert_down": expert_down, "expert_ids": expert_ids, "gate_weights": gate_weights, "grad_out": grad_out}


def silu_parts(values):
    sigmoid_v = jax.nn.sigmoid(values)
    return (values * sigmoid_v, sigmoid_v * (1.0 + values * (1.0 - sigmoid_v)))

def block_sum(pairs):
    quarter = HE // N_TP
    summed = None
    for act_part, matrix in pairs:
        rows_total = act_part.shape[0]
        left_side = act_part.astype(jnp.float32).reshape(rows_total, N_TP, quarter)
        right_side = matrix.astype(jnp.float32).reshape(D, N_TP, quarter)
        product = jnp.einsum('rqh,dqh->rqd', left_side, right_side, precision=lax.Precision.HIGHEST)
        summed = product if summed is None else summed + product
    rounded = lax.optimization_barrier(summed.astype(jnp.bfloat16)).astype(jnp.float32)
    return lax.optimization_barrier(jnp.sum(rounded, axis=1))

def reference(tokens, norm_gain, dense_weight, expert_gate_up, expert_down, expert_ids, gate_weights, grad_out):
    float_in = tokens.astype(jnp.float32)
    inverse = lax.rsqrt(lax.optimization_barrier(jnp.mean(float_in * float_in, axis=1, keepdims=True)) + 1e-05)
    normed = float_in * inverse
    hidden_in = (normed * norm_gain).astype(jnp.bfloat16)
    dense_gate = jnp.dot(hidden_in, dense_weight[0], preferred_element_type=jnp.float32)
    dense_up = jnp.dot(hidden_in, dense_weight[1], preferred_element_type=jnp.float32)
    dense_silu, dense_slope = silu_parts(dense_gate)
    dense_act = (dense_silu * dense_up).astype(jnp.bfloat16)
    dense_out = jnp.dot(dense_act, dense_weight[2].T, preferred_element_type=jnp.float32)
    dense_grad_act = jnp.dot(grad_out, dense_weight[2], preferred_element_type=jnp.float32)
    dense_grad_gate = (dense_grad_act * dense_up * dense_slope).astype(jnp.bfloat16)
    dense_grad_up = (dense_grad_act * dense_silu).astype(jnp.bfloat16)
    dense_grad_in = jnp.dot(dense_grad_gate, dense_weight[0].T, preferred_element_type=jnp.float32)
    dense_grad_in = dense_grad_in + jnp.dot(dense_grad_up, dense_weight[1].T, preferred_element_type=jnp.float32)
    flat_ids = expert_ids.reshape(-1)
    slot_total = flat_ids.shape[0]
    onehot = (flat_ids[:, None] == jnp.arange(EXPERTS, dtype=jnp.int32)[None, :]).astype(jnp.int32)
    ranking = lax.optimization_barrier(jnp.sum((jnp.cumsum(onehot, axis=0) - onehot) * onehot, axis=1))
    slot_bound = N_OUTER * N_EP * MOST
    places = flat_ids * slot_bound + ranking
    slot_index = jnp.zeros((EXPERTS * slot_bound,), jnp.int32).at[places].set(jnp.arange(slot_total, dtype=jnp.int32))
    slot_live = jnp.zeros((EXPERTS * slot_bound,), jnp.float32).at[places].set(1.0)
    gate_flat = gate_weights.reshape(-1)

    def per_expert(carried, inputs):
        moe_out, moe_grad = carried
        gate_up, down_matrix, expert_index = inputs
        start = (expert_index * slot_bound).astype(jnp.int32)
        slot_picks = lax.dynamic_slice_in_dim(slot_index, start, slot_bound)
        live_mask = lax.dynamic_slice_in_dim(slot_live, start, slot_bound)
        rows_token = slot_picks // 2
        weight = jnp.take(gate_flat, slot_picks) * live_mask
        rows_in = jnp.take(hidden_in, rows_token, axis=0)
        expert_gate = jnp.dot(rows_in, gate_up[0], preferred_element_type=jnp.float32)
        expert_up = jnp.dot(rows_in, gate_up[1], preferred_element_type=jnp.float32)
        expert_silu, expert_slope = silu_parts(expert_gate)
        expert_act = (expert_silu * expert_up).astype(jnp.bfloat16)
        pieces = block_sum([(expert_act, down_matrix)])
        moe_out = moe_out.at[rows_token].add(weight[:, None] * pieces)
        rows_grad = jnp.take(grad_out, rows_token, axis=0)
        expert_grad_act = jnp.dot(rows_grad, down_matrix, preferred_element_type=jnp.float32)
        expert_grad_gate = (expert_grad_act * expert_up * expert_slope).astype(jnp.bfloat16)
        expert_grad_up = (expert_grad_act * expert_silu).astype(jnp.bfloat16)
        grad_pieces = block_sum([(expert_grad_gate, gate_up[0]), (expert_grad_up, gate_up[1])])
        moe_grad = moe_grad.at[rows_token].add(weight[:, None] * grad_pieces)
        return ((moe_out, moe_grad), None)
    zeros_out = jnp.zeros((TOKENS, D), jnp.float32)
    (moe_out, moe_grad), unused = lax.scan(per_expert, (zeros_out, zeros_out), (expert_gate_up, expert_down, jnp.arange(EXPERTS, dtype=jnp.int32)))
    layer_out = (float_in + dense_out + moe_out).astype(jnp.bfloat16)
    normed_grad = dense_grad_in + moe_grad
    scaled = normed_grad * norm_gain
    project = lax.optimization_barrier(jnp.mean(scaled * normed, axis=1, keepdims=True))
    grad_in = (grad_out.astype(jnp.float32) + inverse * (scaled - normed * project)).astype(jnp.bfloat16)
    return (layer_out, grad_in)
```

```python
import jax
import jax.numpy as jnp
from jax import lax
from jax.experimental import pallas as pl
from jax.experimental.pallas import tpu as pltpu
from jax.sharding import PartitionSpec as P

MESH = pl.DeviceIdType.MESH
F32 = jnp.float32
BF16 = jnp.bfloat16
ROWS = 128
D = 3584
FF = 640
EP = 16
TP = 4
MOST = 24
SLOTS = EP * MOST
QUARTER = D // TP
HALF = D // 2
OWN = ROWS // TP
CHUNK = 256
EPS = 1e-05
STEPS = [(dz, dx) for dz in (0, 1, 3, 2) for dx in range(4) if (dz, dx) != (0, 0)]
GROUPS = (0, 1, 3, 2)


def silu_parts(values):
    sigmoid_v = jax.nn.sigmoid(values)
    return (values * sigmoid_v, sigmoid_v * (1.0 + values * (1.0 - sigmoid_v)))


def dot(left, right):
    return jnp.dot(left, right, preferred_element_type=F32)


def dot_t(left, right):
    return lax.dot_general(left, right, (((1,), (1,)), ((), ())), preferred_element_type=F32)


def kernel(
    tok, gain, dense_hbm, gate_up_hbm, down_hbm, ids, weights, grad,
    layer_out, grad_in,
    dense_w, gate_up, down, hid, send_h, send_g, rows_h, rows_g, mat_x,
    acc_gate, acc_up, acc_grad, act, dense_out, dense_grad,
    piece_o, piece_g, back_o, back_g, part_o, part_g, red_o, red_g, total_g,
    pick_hi, pick_lo,
    load_sem, core_s, core_r, disp_s, disp_r, ring_s, ring_r, fwd_s, fwd_r,
    self_sem, ret_s, ret_r, red_s, red_r, gat_s, gat_r,
):
    pod, me, tp = lax.axis_index("outer"), lax.axis_index("ep"), lax.axis_index("tp")
    z, x = me // 4, lax.rem(me, 4)
    right, left = lax.rem(tp + 1, TP), lax.rem(tp + 3, TP)

    def expert_at(dz, dx):
        return lax.rem(z + dz + 4, 4) * 4 + lax.rem(x + dx + 4, 4)

    barrier = pltpu.get_barrier_semaphore()
    for dz, dx in STEPS:
        pl.semaphore_signal(barrier, inc=1, device_id=(pod, expert_at(dz, dx), tp), device_id_type=MESH)
    for d in (1, 2, 3):
        pl.semaphore_signal(barrier, inc=1, device_id=(pod, me, lax.rem(tp + d, TP)), device_id_type=MESH)
    pl.semaphore_signal(barrier, inc=1, device_id=(1 - pod, me, tp), device_id_type=MESH)

    loads = [
        pltpu.make_async_copy(gate_up_hbm.at[0], gate_up, load_sem.at[0]),
        pltpu.make_async_copy(down_hbm.at[0], down, load_sem.at[1]),
    ]
    own_rows = pl.ds(pl.multiple_of(pod * HALF, HALF), HALF)
    other_rows = pl.ds(pl.multiple_of((1 - pod) * HALF, HALF), HALF)
    dense_loads = [
        pltpu.make_async_copy(dense_hbm.at[i], dense_w.at[i, own_rows], load_sem.at[2 + i])
        for i in range(3)
    ]
    for load in loads + dense_loads:
        load.start()

    float_in = tok[...].astype(F32)
    inverse = lax.rsqrt(jnp.mean(float_in * float_in, axis=1, keepdims=True) + EPS)
    hid[...] = (float_in * inverse * gain[...]).astype(BF16)

    lanes = lax.broadcasted_iota(jnp.int32, (ROWS, EP), 1)
    first = (ids[:, 0:1] == lanes).astype(F32)
    second = (ids[:, 1:2] == lanes).astype(F32)
    named = first + second
    below = (
        lax.broadcasted_iota(jnp.int32, (ROWS, ROWS), 0)
        > lax.broadcasted_iota(jnp.int32, (ROWS, ROWS), 1)
    ).astype(F32).astype(BF16)
    rank = dot(below, named.astype(BF16))
    slot = lax.broadcasted_iota(jnp.int32, (EP, SLOTS), 1)
    low = lax.broadcasted_iota(jnp.int32, (EP, SLOTS), 0) * MOST
    spread = ((slot >= low) & (slot < low + MOST)).astype(F32).astype(BF16)
    slot_f = lax.broadcasted_iota(jnp.int32, (ROWS, SLOTS), 1).astype(F32)
    within = slot_f - MOST * jnp.floor((slot_f + 0.5) * (1.0 / MOST))
    named_at = dot(named.astype(BF16), spread)
    rank_at = dot(rank.astype(BF16), spread)
    chosen = jnp.where((named_at > 0.5) & (jnp.abs(rank_at - within) < 0.5), 1.0, 0.0)
    weight = first * weights[:, 0:1] + second * weights[:, 1:2]
    weight_hi = weight.astype(BF16)
    weight_lo = (weight - weight_hi.astype(F32)).astype(BF16)
    pick_hi[...] = (chosen * dot(weight_hi, spread)).astype(BF16)
    pick_lo[...] = (chosen * dot(weight_lo, spread)).astype(BF16)
    gather = jnp.transpose(chosen).astype(BF16)

    quarter = pl.ds(pl.multiple_of(tp * QUARTER, 128), QUARTER)
    send_h[...] = dot(gather, hid[:, quarter]).reshape(EP, MOST, QUARTER).astype(BF16)

    def remote(src, dst, send, recv, device):
        return pltpu.make_async_remote_copy(
            src_ref=src, dst_ref=dst, send_sem=send, recv_sem=recv, device_id=device, device_id_type=MESH
        )

    def dispatch(a, send, rows):
        out = []
        for i, (dz, dx) in enumerate(STEPS):
            peer = expert_at(dz, dx)
            out.append(remote(send.at[peer], rows.at[tp, me], disp_s.at[a, i], disp_r.at[a, i], (pod, peer, tp)))
        for copy in out:
            copy.start()
        own = pltpu.make_async_copy(send.at[me], rows.at[tp, me], self_sem.at[a])
        own.start()
        return out, own

    pl.semaphore_wait(barrier, len(STEPS) + 4)
    sent_h, own_h = dispatch(0, send_h, rows_h)
    sent_core = [
        remote(dense_hbm.at[i], dense_w.at[i, own_rows], core_s.at[i], core_r.at[i], (1 - pod, me, tp))
        for i in range(3)
    ]
    for copy in sent_core:
        copy.start()
    send_g[...] = dot(gather, grad[:, quarter]).reshape(EP, MOST, QUARTER).astype(BF16)
    sent_g, own_g = dispatch(1, send_g, rows_g)

    def group_of(rows, q, dz):
        at = pl.multiple_of(lax.rem(z - dz + 4, 4) * 4, 4)
        return rows.at[q, pl.ds(at, 4)]

    def ring_out(a, rows, own):
        out = []
        own.wait()
        for n, group in enumerate(GROUPS):
            for i, (dz, dx) in enumerate(STEPS):
                if dz == group:
                    landed = rows.at[tp, expert_at(-dz, -dx)]
                    remote(landed, landed, disp_s.at[a, i], disp_r.at[a, i], (pod, expert_at(-dz, -dx), tp)).wait_recv()
            block = group_of(rows, tp, group)
            for way, peer in ((0, right), (1, left)):
                copy = remote(block, block, ring_s.at[a, way, n], ring_r.at[a, way, n], (pod, me, peer))
                copy.start()
                out.append(copy)
        return out

    def ring_on(a, rows):
        out = []
        for n, group in enumerate(GROUPS):
            for way, source, peer in ((0, left, right), (1, right, left)):
                block = group_of(rows, source, group)
                remote(block, block, ring_s.at[a, way, n], ring_r.at[a, way, n], (pod, me, source)).wait_recv()
                if n // 2 == way:
                    copy = remote(block, block, fwd_s.at[a, way, n % 2], fwd_r.at[a, way, n % 2], (pod, me, peer))
                    copy.start()
                    out.append(copy)
        return out

    def ring_end(a, rows):
        far = lax.rem(tp + 2, TP)
        for n, group in enumerate(GROUPS):
            way = n // 2
            block = group_of(rows, far, group)
            remote(block, block, fwd_s.at[a, way, n % 2], fwd_r.at[a, way, n % 2], (pod, me, far)).wait_recv()

    def pack(rows, q):
        def step(i, carry):
            block = rows[q, pl.ds(2 * i, 2)]
            mat_x[pl.ds(pl.multiple_of(i * 2 * MOST, 16), 2 * MOST), :] = (
                block.astype(F32).reshape(2 * MOST, QUARTER).astype(BF16)
            )
            return carry

        lax.fori_loop(0, EP // 2, step, 0)

    def forward_quarter(q, start):
        pack(rows_h, q)
        at = pl.ds(pl.multiple_of(q * QUARTER, QUARTER), QUARTER)
        if start:
            acc_gate[...] = dot(mat_x[...], gate_up[0, at, :])
            acc_up[...] = dot(mat_x[...], gate_up[1, at, :])
        else:
            acc_gate[...] += dot(mat_x[...], gate_up[0, at, :])
            acc_up[...] += dot(mat_x[...], gate_up[1, at, :])

    def backward_quarter(q, start):
        pack(rows_g, q)
        at = pl.ds(pl.multiple_of(q * QUARTER, QUARTER), QUARTER)
        if start:
            acc_grad[...] = dot(mat_x[...], down[at, :])
        else:
            acc_grad[...] += dot(mat_x[...], down[at, :])

    ring_h = ring_out(0, rows_h, own_h)
    for load in loads:
        load.wait()
    forward_quarter(tp, True)
    on_h = ring_on(0, rows_h)
    ring_g = ring_out(1, rows_g, own_g)
    forward_quarter(left, False)
    forward_quarter(right, False)
    ring_end(0, rows_h)
    forward_quarter(lax.rem(tp + 2, TP), False)

    silu, slope = silu_parts(acc_gate[...])
    act[0] = (silu * acc_up[...]).astype(BF16)

    def send_back(a, c, piece, back):
        out = []
        for i, (dz, dx) in enumerate(STEPS):
            peer = expert_at(dz, dx)
            out.append(
                remote(piece.at[c, peer], back.at[c, me], ret_s.at[a, c, i], ret_r.at[a, c, i], (pod, peer, tp))
            )
        for copy in out:
            copy.start()
        own = pltpu.make_async_copy(piece.at[c, me], back.at[c, me], self_sem.at[2 + 2 * a + c])
        own.start()
        return out, own

    def columns(c, n):
        return pl.ds(pl.multiple_of(c * HALF + n * CHUNK, CHUNK), CHUNK)

    def within_half(n):
        return pl.ds(pl.multiple_of(n * CHUNK, CHUNK), CHUNK)

    returned_o = []
    for c in range(2):
        def out_step(n, carry):
            piece = dot_t(act[0], down[columns(c, n), :])
            piece_o[c, :, :, within_half(n)] = piece.reshape(EP, MOST, CHUNK).astype(BF16)
            return carry

        lax.fori_loop(0, HALF // CHUNK, out_step, 0)
        returned_o.append(send_back(0, c, piece_o, back_o))

    on_g = ring_on(1, rows_g)

    for load in dense_loads:
        load.wait()
    for i in range(3):
        landed = dense_w.at[i, other_rows]
        remote(dense_hbm.at[i], landed, core_s.at[i], core_r.at[i], (1 - pod, me, tp)).wait_recv()

    wide = 512

    def dense_in_step(n, carry):
        gate, up, back = carry
        at = pl.ds(pl.multiple_of(n * wide, wide), wide)
        gate = gate + dot(hid[:, at], dense_w[0, at, :])
        up = up + dot(hid[:, at], dense_w[1, at, :])
        back = back + dot(grad[:, at], dense_w[2, at, :])
        return gate, up, back

    zeros = jnp.zeros((ROWS, FF), F32)
    d_gate, d_up, d_back = lax.fori_loop(0, D // wide, dense_in_step, (zeros, zeros, zeros))
    d_silu, d_slope = silu_parts(d_gate)
    d_act = (d_silu * d_up).astype(BF16)
    d_grad_gate = (d_back * d_up * d_slope).astype(BF16)
    d_grad_up = (d_back * d_silu).astype(BF16)

    def dense_out_step(n, carry):
        at = pl.ds(pl.multiple_of(n * CHUNK, CHUNK), CHUNK)
        dense_out[:, at] = dot_t(d_act, dense_w[2, at, :])
        dense_grad[:, at] = dot_t(d_grad_gate, dense_w[0, at, :]) + dot_t(d_grad_up, dense_w[1, at, :])
        return carry

    lax.fori_loop(0, D // CHUNK, dense_out_step, 0)

    backward_quarter(tp, True)
    backward_quarter(left, False)
    backward_quarter(right, False)
    ring_end(1, rows_g)
    backward_quarter(lax.rem(tp + 2, TP), False)
    silu, slope = silu_parts(acc_gate[...])
    act[0] = (acc_grad[...] * acc_up[...] * slope).astype(BF16)
    act[1] = (acc_grad[...] * silu).astype(BF16)
    for copies, own in returned_o:
        for copy in copies:
            copy.wait_send()
    returned_g = []
    for c in range(2):
        def grad_step(n, carry):
            at = columns(c, n)
            piece = dot_t(act[0], gate_up[0, at, :]) + dot_t(act[1], gate_up[1, at, :])
            piece_g[c, :, :, within_half(n)] = piece.reshape(EP, MOST, CHUNK).astype(BF16)
            return carry

        lax.fori_loop(0, HALF // CHUNK, grad_step, 0)
        returned_g.append(send_back(1, c, piece_g, back_g))

    mine = pl.ds(pl.multiple_of(tp * OWN, OWN), OWN)

    def combine(a, c, returned, back, dense, part, red):
        returned[c][1].wait()
        for i, (dz, dx) in enumerate(STEPS):
            source = expert_at(-dz, -dx)
            landed = back.at[c, source]
            remote(landed, landed, ret_s.at[a, c, i], ret_r.at[a, c, i], (pod, source, tp)).wait_recv()

        def step(n, carry):
            rows = back[c, :, :, within_half(n)].astype(F32).reshape(SLOTS, CHUNK).astype(BF16)
            at = columns(c, n)
            total = dense[:, at] + dot(pick_hi[...], rows) + dot(pick_lo[...], rows)
            part[c, :, within_half(n)] = total.astype(BF16)
            return carry

        lax.fori_loop(0, HALF // CHUNK, step, 0)
        out = []
        for d in (2, 1, 3):
            peer = lax.rem(tp + d, TP)
            rows_at = pl.ds(pl.multiple_of(peer * OWN, OWN), OWN)
            copy = remote(part.at[c, rows_at], red.at[c, d - 1], red_s.at[a, c, d - 1], red_r.at[a, c, d - 1], (pod, me, peer))
            copy.start()
            out.append(copy)
        return out

    def reduced(a, c, part, red):
        total = part[c, mine, :].astype(F32)
        for d in (1, 2, 3):
            landed = red.at[c, d - 1]
            peer = lax.rem(tp + d, TP)
            remote(landed, landed, red_s.at[a, c, d - 1], red_r.at[a, c, d - 1], (pod, me, peer)).wait_recv()
            total = total + red[c, d - 1].astype(F32)
        return total

    def spread_out(k, ref):
        out = []
        for d in (2, 1, 3):
            peer = lax.rem(tp + d, TP)
            copy = remote(ref, ref, gat_s.at[k, d - 1], gat_r.at[k, d - 1], (pod, me, peer))
            copy.start()
            out.append(copy)
        return out

    def gathered(k, ref, c):
        for d in (1, 2, 3):
            source = lax.rem(tp + 4 - d, TP)
            rows_at = pl.ds(pl.multiple_of(source * OWN, OWN), OWN)
            landed = ref.at[rows_at] if c is None else ref.at[rows_at, pl.ds(c * HALF, HALF)]
            remote(landed, landed, gat_s.at[k, d - 1], gat_r.at[k, d - 1], (pod, me, source)).wait_recv()

    pending = []
    for c in range(2):
        pending += combine(0, c, returned_o, back_o, dense_out, part_o, red_o)
    for c in range(2):
        half = pl.ds(c * HALF, HALF)
        total = reduced(0, c, part_o, red_o)
        layer_out[mine, half] = (tok[mine, half].astype(F32) + total).astype(BF16)
        pending += spread_out(c, layer_out.at[mine, half])
    for c in range(2):
        pending += combine(1, c, returned_g, back_g, dense_grad, part_g, red_g)
    for c in range(2):
        total_g[:, pl.ds(c * HALF, HALF)] = reduced(1, c, part_g, red_g)
    own_in = tok[mine, :].astype(F32)
    own_inverse = lax.rsqrt(jnp.mean(own_in * own_in, axis=1, keepdims=True) + EPS)
    normed = own_in * own_inverse
    scaled = total_g[...] * gain[...]
    project = jnp.mean(scaled * normed, axis=1, keepdims=True)
    grad_in[mine, :] = (
        grad[mine, :].astype(F32) + own_inverse * (scaled - normed * project)
    ).astype(BF16)
    pending += spread_out(2, grad_in.at[mine])
    gathered(0, layer_out, 0)
    gathered(1, layer_out, 1)
    gathered(2, grad_in, None)
    for copies, own in returned_g:
        pending += copies
    for copy in pending + sent_h + sent_g + sent_core + ring_h + ring_g + on_h + on_g:
        copy.wait_send()


def body(tokens, norm_gain, dense_weight, expert_gate_up, expert_down, expert_ids, gate_weights, grad_out):
    vmem = pl.BlockSpec(memory_space=pltpu.VMEM)
    hbm = pl.BlockSpec(memory_space=pl.ANY)
    dma = pltpu.SemaphoreType.DMA
    steps = len(STEPS)
    row_shape = jax.ShapeDtypeStruct((ROWS, D), BF16)
    return pl.pallas_call(
        kernel,
        name="layer",
        out_shape=[row_shape, row_shape],
        in_specs=[vmem, vmem, hbm, hbm, hbm, vmem, vmem, vmem],
        out_specs=[vmem, vmem],
        scratch_shapes=[
            pltpu.VMEM((3, D, FF), BF16),
            pltpu.VMEM((2, D, FF), BF16),
            pltpu.VMEM((D, FF), BF16),
            pltpu.VMEM((ROWS, D), BF16),
            pltpu.VMEM((EP, MOST, QUARTER), BF16),
            pltpu.VMEM((EP, MOST, QUARTER), BF16),
            pltpu.VMEM((TP, EP, MOST, QUARTER), BF16),
            pltpu.VMEM((TP, EP, MOST, QUARTER), BF16),
            pltpu.VMEM((SLOTS, QUARTER), BF16),
            pltpu.VMEM((SLOTS, FF), F32),
            pltpu.VMEM((SLOTS, FF), F32),
            pltpu.VMEM((SLOTS, FF), F32),
            pltpu.VMEM((2, SLOTS, FF), BF16),
            pltpu.VMEM((ROWS, D), F32),
            pltpu.VMEM((ROWS, D), F32),
            pltpu.VMEM((2, EP, MOST, HALF), BF16),
            pltpu.VMEM((2, EP, MOST, HALF), BF16),
            pltpu.VMEM((2, EP, MOST, HALF), BF16),
            pltpu.VMEM((2, EP, MOST, HALF), BF16),
            pltpu.VMEM((2, ROWS, HALF), BF16),
            pltpu.VMEM((2, ROWS, HALF), BF16),
            pltpu.VMEM((2, 3, OWN, HALF), BF16),
            pltpu.VMEM((2, 3, OWN, HALF), BF16),
            pltpu.VMEM((OWN, D), F32),
            pltpu.VMEM((ROWS, SLOTS), BF16),
            pltpu.VMEM((ROWS, SLOTS), BF16),
            dma((5,)),
            dma((3,)),
            dma((3,)),
            dma((2, steps)),
            dma((2, steps)),
            dma((2, 2, 4)),
            dma((2, 2, 4)),
            dma((2, 2, 2)),
            dma((2, 2, 2)),
            dma((6,)),
            dma((2, 2, steps)),
            dma((2, 2, steps)),
            dma((2, 2, 3)),
            dma((2, 2, 3)),
            dma((3, 3)),
            dma((3, 3)),
        ],
        compiler_params=pltpu.CompilerParams(
            collective_id=0, has_side_effects=True, vmem_limit_bytes=63 * 2**20
        ),
    )(
        tokens, norm_gain.reshape(1, D), dense_weight, expert_gate_up, expert_down,
        expert_ids, gate_weights, grad_out,
    )


def solution(mesh):
    rows = P(("outer", "ep"), None)
    in_specs = (rows, P(), P(None, "outer", "tp"), P("ep", None, None, "tp"), P("ep", None, "tp"), rows, rows, rows)
    return jax.shard_map(body, mesh=mesh, in_specs=in_specs, out_specs=(rows, rows), check_vma=False)
```

```python
import jax
import jax.numpy as jnp
from jax import lax
from jax.experimental import pallas as pl
from jax.experimental.pallas import tpu as pltpu
from jax.sharding import PartitionSpec as P

MESH = pl.DeviceIdType.MESH
F32 = jnp.float32
BF16 = jnp.bfloat16
ROWS = 128
D = 3584
FF = 640
EP = 16
TP = 4
MOST = 24
SLOTS = EP * MOST
QUARTER = D // TP
RING_H = 640
DIRECT = D - TP * RING_H
HALF = D // 2
PARTS = 4
PART = D // PARTS
OWN = ROWS // TP
EPS = 1e-05
STEPS = [(dz, dx) for dz in (0, 1, 3, 2) for dx in range(4) if (dz, dx) != (0, 0)]
GROUPS = (0, 1, 3, 2)


def silu_parts(values):
    sigmoid_v = jax.nn.sigmoid(values)
    return (values * sigmoid_v, sigmoid_v * (1.0 + values * (1.0 - sigmoid_v)))


def dot(left, right):
    return jnp.dot(left, right, preferred_element_type=F32)


def dot_t(left, right):
    return lax.dot_general(left, right, (((1,), (1,)), ((), ())), preferred_element_type=F32)


def kernel(
    tok, gain, dense_hbm, gate_up_hbm, down_hbm, ids, weights, grad,
    layer_out, grad_in,
    dense_w, gate_up, down, hid, send_h, send_d, send_g, rows_h, rows_d, rows_g, mat_x,
    acc_gate, acc_up, acc_grad, act, dense_out, dense_grad,
    piece_o, piece_g, back_o, back_g, part_o, part_g, red_o, red_g, total_g,
    picks, dense_acc,
    load_sem, core_s, core_r, disp_s, disp_r, ring_s, ring_r, fwd_s, fwd_r,
    self_sem, ret_s, ret_r, red_s, red_r, gat_s, gat_r,
):
    pod, me, tp = lax.axis_index("outer"), lax.axis_index("ep"), lax.axis_index("tp")
    z, x = me // 4, lax.rem(me, 4)
    right, left = lax.rem(tp + 1, TP), lax.rem(tp + 3, TP)

    def expert_at(dz, dx):
        return lax.rem(z + dz + 4, 4) * 4 + lax.rem(x + dx + 4, 4)

    barrier = pltpu.get_barrier_semaphore()
    for dz, dx in STEPS:
        pl.semaphore_signal(barrier, inc=1, device_id=(pod, expert_at(dz, dx), tp), device_id_type=MESH)
    for d in (1, 2, 3):
        pl.semaphore_signal(barrier, inc=1, device_id=(pod, me, lax.rem(tp + d, TP)), device_id_type=MESH)
    pl.semaphore_signal(barrier, inc=1, device_id=(1 - pod, me, tp), device_id_type=MESH)

    loads = [
        pltpu.make_async_copy(gate_up_hbm.at[0], gate_up, load_sem.at[0]),
        pltpu.make_async_copy(down_hbm.at[0], down, load_sem.at[1]),
    ]
    own_rows = pl.ds(pl.multiple_of(pod * HALF, HALF), HALF)
    other_rows = pl.ds(pl.multiple_of((1 - pod) * HALF, HALF), HALF)
    dense_loads = [
        pltpu.make_async_copy(dense_hbm.at[i], dense_w.at[i, own_rows], load_sem.at[2 + i])
        for i in range(3)
    ]
    for load in loads + dense_loads:
        load.start()

    float_in = tok[...].astype(F32)
    inverse = lax.rsqrt(jnp.mean(float_in * float_in, axis=1, keepdims=True) + EPS)
    hid[...] = (float_in * inverse * gain[...].reshape(1, D)).astype(BF16)

    experts = lax.broadcasted_iota(jnp.int32, (EP, ROWS), 0)
    first = (ids[0:1, :] == experts).astype(F32)
    second = (ids[1:2, :] == experts).astype(F32)
    named = (first + second).astype(BF16)
    before = (
        lax.broadcasted_iota(jnp.int32, (ROWS, ROWS), 0)
        < lax.broadcasted_iota(jnp.int32, (ROWS, ROWS), 1)
    ).astype(F32).astype(BF16)
    rank = dot(named, before)
    slot = lax.broadcasted_iota(jnp.int32, (SLOTS, EP), 0)
    low = lax.broadcasted_iota(jnp.int32, (SLOTS, EP), 1) * MOST
    spread = ((slot >= low) & (slot < low + MOST)).astype(F32).astype(BF16)
    slot_f = lax.broadcasted_iota(jnp.int32, (SLOTS, ROWS), 0).astype(F32)
    within = slot_f - MOST * jnp.floor((slot_f + 0.5) * (1.0 / MOST))
    named_at = dot(spread, named)
    rank_at = dot(spread, rank.astype(BF16))
    chosen = jnp.where((named_at > 0.5) & (jnp.abs(rank_at - within) < 0.5), 1.0, 0.0)
    gather = chosen.astype(BF16)

    def pick_rows(source, start, width):
        at = pl.ds(pl.multiple_of(start, 128), width)
        return dot(gather, source[:, at]).reshape(EP, MOST, width).astype(BF16)

    send_h[...] = pick_rows(hid, tp * RING_H, RING_H)

    def make_picks():
        weight = first * weights[0:1, :] + second * weights[1:2, :]
        weight_hi = weight.astype(BF16)
        weight_lo = (weight - weight_hi.astype(F32)).astype(BF16)
        picks[0:ROWS, :] = jnp.transpose(chosen * dot(spread, weight_hi)).astype(BF16)
        picks[ROWS:, :] = jnp.transpose(chosen * dot(spread, weight_lo)).astype(BF16)

    def remote(src, dst, send, recv, device):
        return pltpu.make_async_remote_copy(
            src_ref=src, dst_ref=dst, send_sem=send, recv_sem=recv, device_id=device, device_id_type=MESH
        )

    def dispatch(a, send, rows):
        out = []
        for i, (dz, dx) in enumerate(STEPS):
            peer = expert_at(dz, dx)
            out.append(remote(send.at[peer], rows.at[me], disp_s.at[a, i], disp_r.at[a, i], (pod, peer, tp)))
        for copy in out:
            copy.start()
        own = pltpu.make_async_copy(send.at[me], rows.at[me], self_sem.at[a])
        own.start()
        return out, own

    def dispatched(a, rows, i):
        dz, dx = STEPS[i]
        source = expert_at(-dz, -dx)
        landed = rows.at[source]
        remote(landed, landed, disp_s.at[a, i], disp_r.at[a, i], (pod, source, tp)).wait_recv()

    pl.semaphore_wait(barrier, len(STEPS) + 4)
    sent_h, own_h = dispatch(0, send_h, rows_h.at[tp])
    sent_core = [
        remote(dense_hbm.at[i], dense_w.at[i, own_rows], core_s.at[i], core_r.at[i], (1 - pod, me, tp))
        for i in range(3)
    ]
    for copy in sent_core:
        copy.start()
    send_d[...] = pick_rows(hid, TP * RING_H, DIRECT)
    sent_d, own_d = dispatch(2, send_d, rows_d)
    send_g[...] = pick_rows(grad, tp * QUARTER, QUARTER)
    sent_g, own_g = dispatch(1, send_g, rows_g.at[tp])

    def group_of(rows, q, dz):
        at = pl.multiple_of(lax.rem(z - dz + 4, 4) * 4, 4)
        return rows.at[q, pl.ds(at, 4)]

    def ring_out(a, rows, own):
        out = []
        own.wait()
        for n, group in enumerate(GROUPS):
            for i, (dz, dx) in enumerate(STEPS):
                if dz == group:
                    dispatched(a, rows.at[tp], i)
            block = group_of(rows, tp, group)
            for way, peer in ((0, right), (1, left)):
                copy = remote(block, block, ring_s.at[a, way, n], ring_r.at[a, way, n], (pod, me, peer))
                copy.start()
                out.append(copy)
        return out

    def ring_on(a, rows, way):
        source, peer = ((left, right), (right, left))[way]
        out = []
        for n in (2 * way, 2 * way + 1):
            block = group_of(rows, source, GROUPS[n])
            remote(block, block, ring_s.at[a, way, n], ring_r.at[a, way, n], (pod, me, source)).wait_recv()
            copy = remote(block, block, fwd_s.at[a, way, n % 2], fwd_r.at[a, way, n % 2], (pod, me, peer))
            copy.start()
            out.append(copy)
        return out

    def ring_in(a, rows, way):
        source = (left, right)[way]
        for n in (2 - 2 * way, 3 - 2 * way):
            block = group_of(rows, source, GROUPS[n])
            remote(block, block, ring_s.at[a, way, n], ring_r.at[a, way, n], (pod, me, source)).wait_recv()

    def ring_end(a, rows):
        far = lax.rem(tp + 2, TP)
        for n, group in enumerate(GROUPS):
            way = n // 2
            block = group_of(rows, far, group)
            remote(block, block, fwd_s.at[a, way, n % 2], fwd_r.at[a, way, n % 2], (pod, me, far)).wait_recv()

    def pack(rows, width):
        def step(i, carry):
            block = rows[pl.ds(2 * i, 2)]
            mat_x[pl.ds(pl.multiple_of(i * 2 * MOST, 16), 2 * MOST), 0:width] = (
                block.astype(F32).reshape(2 * MOST, width).astype(BF16)
            )
            return carry

        lax.fori_loop(0, EP // 2, step, 0)

    def forward_part(rows, at, width, start):
        pack(rows, width)
        if start:
            acc_gate[...] = dot(mat_x[:, 0:width], gate_up[0, at, :])
            acc_up[...] = dot(mat_x[:, 0:width], gate_up[1, at, :])
        else:
            acc_gate[...] += dot(mat_x[:, 0:width], gate_up[0, at, :])
            acc_up[...] += dot(mat_x[:, 0:width], gate_up[1, at, :])

    def forward_quarter(q, start):
        at = pl.ds(pl.multiple_of(q * RING_H, RING_H), RING_H)
        forward_part(rows_h.at[q], at, RING_H, start)

    def backward_quarter(q, start):
        pack(rows_g.at[q], QUARTER)
        at = pl.ds(pl.multiple_of(q * QUARTER, QUARTER), QUARTER)
        if start:
            acc_grad[...] = dot(mat_x[:, 0:QUARTER], down[at, :])
        else:
            acc_grad[...] += dot(mat_x[:, 0:QUARTER], down[at, :])

    def dense_in(i, which):
        at = (own_rows, other_rows)[which]
        left_side = (hid, hid, grad)[i]
        if which == 0:
            dense_loads[i].wait()
            dense_acc[i] = dot(left_side[:, at], dense_w[i, at, :])
        else:
            dense_acc[i] += dot(left_side[:, at], dense_w[i, at, :])

    def dense_landed(i):
        landed = dense_w.at[i, other_rows]
        remote(dense_hbm.at[i], landed, core_s.at[i], core_r.at[i], (1 - pod, me, tp)).wait_recv()

    for i in range(3):
        dense_in(i, 0)
    ring_h = ring_out(0, rows_h, own_h)
    for load in loads:
        load.wait()
    forward_quarter(tp, True)
    dense_landed(0)
    dense_in(0, 1)
    on_h = ring_on(0, rows_h, 0)
    dense_landed(1)
    dense_in(1, 1)
    on_h += ring_on(0, rows_h, 1)
    ring_in(0, rows_h, 0)
    forward_quarter(left, False)
    ring_in(0, rows_h, 1)
    forward_quarter(right, False)
    own_d.wait()
    for i in range(len(STEPS)):
        dispatched(2, rows_d, i)
    forward_part(rows_d, pl.ds(TP * RING_H, DIRECT), DIRECT, False)
    ring_end(0, rows_h)
    forward_quarter(lax.rem(tp + 2, TP), False)

    silu, slope = silu_parts(acc_gate[...])
    act[0] = (silu * acc_up[...]).astype(BF16)

    def send_back(a, c, piece, back):
        out = []
        for i, (dz, dx) in enumerate(STEPS):
            peer = expert_at(dz, dx)
            out.append(
                remote(piece.at[c, peer], back.at[c, me], ret_s.at[a, c, i], ret_r.at[a, c, i], (pod, peer, tp))
            )
        for copy in out:
            copy.start()
        own = pltpu.make_async_copy(piece.at[c, me], back.at[c, me], self_sem.at[3 + PARTS * a + c])
        own.start()
        return out, own

    returned_o = []
    for c in range(PARTS):
        cols = pl.ds(c * PART, PART)
        piece_o[c] = dot_t(act[0], down[cols, :]).reshape(EP, MOST, PART).astype(BF16)
        returned_o.append(send_back(0, c, piece_o, back_o))
        if c == 0:
            ring_g = ring_out(1, rows_g, own_g)

    dense_landed(2)
    dense_in(2, 1)
    on_g = ring_on(1, rows_g, 0)
    d_silu, d_slope = silu_parts(dense_acc[0])
    d_up, d_back = dense_acc[1], dense_acc[2]
    d_act = (d_silu * d_up).astype(BF16)
    d_grad_gate = (d_back * d_up * d_slope).astype(BF16)
    d_grad_up = (d_back * d_silu).astype(BF16)
    for c in range(2):
        half = pl.ds(c * HALF, HALF)
        dense_out[:, half] = dot_t(d_act, dense_w[2, half, :]).astype(BF16)
    on_g += ring_on(1, rows_g, 1)
    for c in range(2):
        half = pl.ds(c * HALF, HALF)
        total = dot_t(d_grad_gate, dense_w[0, half, :]) + dot_t(d_grad_up, dense_w[1, half, :])
        dense_grad[:, half] = total.astype(BF16)
    make_picks()

    mine = pl.ds(pl.multiple_of(tp * OWN, OWN), OWN)

    def combine(a, c, returned, back, dense, part, red):
        returned[c][1].wait()
        for i, (dz, dx) in enumerate(STEPS):
            source = expert_at(-dz, -dx)
            landed = back.at[c, source]
            remote(landed, landed, ret_s.at[a, c, i], ret_r.at[a, c, i], (pod, source, tp)).wait_recv()

        rows = back[c].astype(F32).reshape(SLOTS, PART).astype(BF16)
        product = dot(picks[...], rows)
        total = dense[:, pl.ds(c * PART, PART)] + product[:ROWS] + product[ROWS:]
        part[c] = total.astype(BF16)
        out = []
        for d in (2, 1, 3):
            peer = lax.rem(tp + d, TP)
            rows_at = pl.ds(pl.multiple_of(peer * OWN, OWN), OWN)
            copy = remote(part.at[c, rows_at], red.at[c, d - 1], red_s.at[a, c, d - 1], red_r.at[a, c, d - 1], (pod, me, peer))
            copy.start()
            out.append(copy)
        return out

    def reduced(a, c, part, red):
        total = part[c, mine, :].astype(F32)
        for d in (1, 2, 3):
            landed = red.at[c, d - 1]
            peer = lax.rem(tp + d, TP)
            remote(landed, landed, red_s.at[a, c, d - 1], red_r.at[a, c, d - 1], (pod, me, peer)).wait_recv()
            total = total + red[c, d - 1].astype(F32)
        return total

    def spread_out(k, ref):
        out = []
        for d in (2, 1, 3):
            peer = lax.rem(tp + d, TP)
            copy = remote(ref, ref, gat_s.at[k, d - 1], gat_r.at[k, d - 1], (pod, me, peer))
            copy.start()
            out.append(copy)
        return out

    def gathered(k, ref, c):
        for d in (1, 2, 3):
            source = lax.rem(tp + 4 - d, TP)
            rows_at = pl.ds(pl.multiple_of(source * OWN, OWN), OWN)
            landed = ref.at[rows_at, pl.ds(c * PART, PART)] if k < PARTS else ref.at[c, rows_at]
            remote(landed, landed, gat_s.at[k, d - 1], gat_r.at[k, d - 1], (pod, me, source)).wait_recv()

    pending = []

    def combine_o(c):
        return combine(0, c, returned_o, back_o, dense_out, part_o, red_o)

    def reduce_o(c):
        cols = pl.ds(c * PART, PART)
        total = reduced(0, c, part_o, red_o)
        layer_out[mine, cols] = (tok[mine, cols].astype(F32) + total).astype(BF16)
        return spread_out(c, layer_out.at[mine, cols])

    backward_quarter(tp, True)
    ring_in(1, rows_g, 0)
    backward_quarter(left, False)
    ring_in(1, rows_g, 1)
    backward_quarter(right, False)
    pending += combine_o(0)
    pending += combine_o(1)
    ring_end(1, rows_g)
    backward_quarter(lax.rem(tp + 2, TP), False)
    silu, slope = silu_parts(acc_gate[...])
    act[0] = (acc_grad[...] * acc_up[...] * slope).astype(BF16)
    act[1] = (acc_grad[...] * silu).astype(BF16)
    returned_g = []
    for c in range(PARTS):
        cols = pl.ds(c * PART, PART)
        piece = dot_t(act[0], gate_up[0, cols, :]) + dot_t(act[1], gate_up[1, cols, :])
        piece_g[c] = piece.reshape(EP, MOST, PART).astype(BF16)
        returned_g.append(send_back(1, c, piece_g, back_g))
        if c == 1:
            pending += reduce_o(0)

    def combine_g(c):
        return combine(1, c, returned_g, back_g, dense_grad, part_g, red_g)

    def reduce_g(c):
        total_g[c, mine] = reduced(1, c, part_g, red_g).astype(BF16)
        return spread_out(PARTS + c, total_g.at[c, mine])

    pending += combine_o(2)
    pending += reduce_o(1)
    pending += combine_o(3)
    pending += reduce_o(2)
    pending += reduce_o(3)
    pending += combine_g(0)
    for c in range(1, PARTS):
        pending += combine_g(c)
        pending += reduce_g(c - 1)
    pending += reduce_g(PARTS - 1)
    project = jnp.zeros((ROWS, 1), F32)
    for c in range(PARTS):
        cols = pl.ds(c * PART, PART)
        gathered(PARTS + c, total_g, c)
        scaled = total_g[c].astype(F32) * gain[cols].reshape(1, PART)
        project += jnp.sum(scaled * (tok[:, cols].astype(F32) * inverse), axis=1, keepdims=True)
    project = project * (1.0 / D)
    for c in range(PARTS):
        cols = pl.ds(c * PART, PART)
        scaled = total_g[c].astype(F32) * gain[cols].reshape(1, PART)
        normed = tok[:, cols].astype(F32) * inverse
        grad_in[:, cols] = (
            grad[:, cols].astype(F32) + inverse * (scaled - normed * project)
        ).astype(BF16)
    for c in range(PARTS):
        gathered(c, layer_out, c)
    for copies, own in returned_o + returned_g:
        pending += copies
    for copy in pending + sent_h + sent_d + sent_g + sent_core + ring_h + ring_g + on_h + on_g:
        copy.wait_send()


def copy_out(first, second, first_out, second_out):
    first_out[...] = first[...]
    second_out[...] = second[...]


def body(tokens, norm_gain, dense_weight, expert_gate_up, expert_down, expert_ids, gate_weights, grad_out):
    vmem = pl.BlockSpec(memory_space=pltpu.VMEM)
    hbm = pl.BlockSpec(memory_space=pl.ANY)
    dma = pltpu.SemaphoreType.DMA
    steps = len(STEPS)
    row_shape = jax.ShapeDtypeStruct((ROWS, D), BF16)
    results = pl.pallas_call(
        kernel,
        name="layer",
        out_shape=[row_shape, row_shape],
        in_specs=[vmem, vmem, hbm, hbm, hbm, vmem, vmem, vmem],
        out_specs=[vmem, vmem],
        scratch_shapes=[
            pltpu.VMEM((3, D, FF), BF16),
            pltpu.VMEM((2, D, FF), BF16),
            pltpu.VMEM((D, FF), BF16),
            pltpu.VMEM((ROWS, D), BF16),
            pltpu.VMEM((EP, MOST, RING_H), BF16),
            pltpu.VMEM((EP, MOST, DIRECT), BF16),
            pltpu.VMEM((EP, MOST, QUARTER), BF16),
            pltpu.VMEM((TP, EP, MOST, RING_H), BF16),
            pltpu.VMEM((EP, MOST, DIRECT), BF16),
            pltpu.VMEM((TP, EP, MOST, QUARTER), BF16),
            pltpu.VMEM((SLOTS, max(DIRECT, QUARTER)), BF16),
            pltpu.VMEM((SLOTS, FF), F32),
            pltpu.VMEM((SLOTS, FF), F32),
            pltpu.VMEM((SLOTS, FF), F32),
            pltpu.VMEM((2, SLOTS, FF), BF16),
            pltpu.VMEM((ROWS, D), BF16),
            pltpu.VMEM((ROWS, D), BF16),
            pltpu.VMEM((PARTS, EP, MOST, PART), BF16),
            pltpu.VMEM((PARTS, EP, MOST, PART), BF16),
            pltpu.VMEM((PARTS, EP, MOST, PART), BF16),
            pltpu.VMEM((PARTS, EP, MOST, PART), BF16),
            pltpu.VMEM((PARTS, ROWS, PART), BF16),
            pltpu.VMEM((PARTS, ROWS, PART), BF16),
            pltpu.VMEM((PARTS, 3, OWN, PART), BF16),
            pltpu.VMEM((PARTS, 3, OWN, PART), BF16),
            pltpu.VMEM((PARTS, ROWS, PART), BF16),
            pltpu.VMEM((2 * ROWS, SLOTS), BF16),
            pltpu.VMEM((3, ROWS, FF), F32),
            dma((5,)),
            dma((3,)),
            dma((3,)),
            dma((3, steps)),
            dma((3, steps)),
            dma((2, 2, 4)),
            dma((2, 2, 4)),
            dma((2, 2, 2)),
            dma((2, 2, 2)),
            dma((3 + 2 * PARTS,)),
            dma((2, PARTS, steps)),
            dma((2, PARTS, steps)),
            dma((2, PARTS, 3)),
            dma((2, PARTS, 3)),
            dma((2 * PARTS, 3)),
            dma((2 * PARTS, 3)),
        ],
        compiler_params=pltpu.CompilerParams(
            collective_id=0, has_side_effects=True, vmem_limit_bytes=63 * 2**20
        ),
    )(
        tokens, norm_gain, dense_weight, expert_gate_up, expert_down,
        expert_ids.T, gate_weights.T, grad_out,
    )
    return pl.pallas_call(
        copy_out,
        name="copy_out",
        out_shape=[row_shape, row_shape],
        in_specs=[vmem, vmem],
        out_specs=[vmem, vmem],
    )(*results)


def solution(mesh):
    rows = P(("outer", "ep"), None)
    in_specs = (rows, P(), P(None, "outer", "tp"), P("ep", None, None, "tp"), P("ep", None, "tp"), rows, rows, rows)
    return jax.shard_map(body, mesh=mesh, in_specs=in_specs, out_specs=(rows, rows), check_vma=False)
```

```python
import jax
import jax.numpy as jnp
from jax import lax
from jax.experimental import pallas as pl
from jax.experimental.pallas import tpu as pltpu
from jax.sharding import PartitionSpec as P

MESH = pl.DeviceIdType.MESH
F32 = jnp.float32
BF16 = jnp.bfloat16
ROWS = 128
D = 3584
FF = 640
EP = 16
TP = 4
MOST = 24
SLOTS = EP * MOST
RING = 640
DIRECT = D - TP * RING
RING_G = 768
DIRECT_G = D - TP * RING_G
HALF = D // 2
PARTS_O = ((0, 896), (896, 896), (1792, 896), (2688, 896))
BLOCK = 256
WHOLE_G = D - TP * BLOCK
PARTS_G = ((0, 1024), (1024, 1024), (2048, WHOLE_G - 2048))
PARTS = 4
OWN = ROWS // TP
EPS = 1e-05
STEPS = [(dz, dx) for dz in (0, 1, 3, 2) for dx in range(4) if (dz, dx) != (0, 0)]
GROUPS = (0, 1, 3, 2)


def silu_parts(values):
    sigmoid_v = jax.nn.sigmoid(values)
    return (values * sigmoid_v, sigmoid_v * (1.0 + values * (1.0 - sigmoid_v)))


def dot(left, right):
    return jnp.dot(left, right, preferred_element_type=F32)


def dot_t(left, right):
    return lax.dot_general(left, right, (((1,), (1,)), ((), ())), preferred_element_type=F32)


def kernel(
    tok, gain, dense_hbm, gate_up_hbm, down_hbm, ids, weights, grad,
    layer_out, total_g,
    dense_w, gate_up, down, hid, send_h, send_g, rows_h, rows_d, rows_g, rows_e, mat_x,
    acc_gate, acc_up, acc_grad, act, dense_out, dense_grad,
    piece_o, piece_g, back_o, back_g, part_o, part_g, red_o, red_g,
    picks, dense_acc, cross_out, cross_in, merged, back_x, dense_in_x,
    load_sem, core_s, core_r, disp_s, ring_s, ring_r, fwd_s, fwd_r, disp_r, direct_r,
    ret_s, ret_r, red_s, red_r, gat_s, gat_r,
    cross_s, cross_r, dense_s, dense_r, retx_s, retx_r,
):
    pod, me, tp = lax.axis_index("outer"), lax.axis_index("ep"), lax.axis_index("tp")
    z, x = me // 4, lax.rem(me, 4)
    right, left = lax.rem(tp + 1, TP), lax.rem(tp + 3, TP)

    def expert_at(dz, dx):
        return lax.rem(z + dz + 4, 4) * 4 + lax.rem(x + dx + 4, 4)

    barrier = pltpu.get_barrier_semaphore()
    for dz, dx in STEPS:
        pl.semaphore_signal(barrier, inc=1, device_id=(pod, expert_at(dz, dx), tp), device_id_type=MESH)
    for d in (1, 2, 3):
        pl.semaphore_signal(barrier, inc=1, device_id=(pod, me, lax.rem(tp + d, TP)), device_id_type=MESH)
    pl.semaphore_signal(barrier, inc=1, device_id=(1 - pod, me, tp), device_id_type=MESH)

    loads = [
        pltpu.make_async_copy(gate_up_hbm.at[0], gate_up, load_sem.at[0]),
        pltpu.make_async_copy(down_hbm.at[0], down, load_sem.at[1]),
    ]
    own_rows = pl.ds(pl.multiple_of(pod * HALF, HALF), HALF)
    other_rows = pl.ds(pl.multiple_of((1 - pod) * HALF, HALF), HALF)
    dense_loads = [
        pltpu.make_async_copy(dense_hbm.at[i], dense_w.at[i, own_rows], load_sem.at[2 + i])
        for i in range(3)
    ]
    for load in loads + dense_loads:
        load.start()

    float_in = tok[...].astype(F32)
    inverse = lax.rsqrt(jnp.mean(float_in * float_in, axis=1, keepdims=True) + EPS)
    hid[...] = (float_in * inverse * gain[...].reshape(1, D)).astype(BF16)

    experts = lax.broadcasted_iota(jnp.int32, (EP, ROWS), 0)
    first = (ids[0:1, :] == experts).astype(F32)
    second = (ids[1:2, :] == experts).astype(F32)
    named = (first + second).astype(BF16)
    before = (
        lax.broadcasted_iota(jnp.int32, (ROWS, ROWS), 0)
        < lax.broadcasted_iota(jnp.int32, (ROWS, ROWS), 1)
    ).astype(F32).astype(BF16)
    rank = dot(named, before)
    slot = lax.broadcasted_iota(jnp.int32, (SLOTS, EP), 0)
    low = lax.broadcasted_iota(jnp.int32, (SLOTS, EP), 1) * MOST
    spread = ((slot >= low) & (slot < low + MOST)).astype(F32).astype(BF16)
    slot_f = lax.broadcasted_iota(jnp.int32, (SLOTS, ROWS), 0).astype(F32)
    within = slot_f - MOST * jnp.floor((slot_f + 0.5) * (1.0 / MOST))
    named_at = dot(spread, named)
    rank_at = dot(spread, rank.astype(BF16))
    chosen = jnp.where((named_at > 0.5) & (jnp.abs(rank_at - within) < 0.5), 1.0, 0.0)
    gather = chosen.astype(BF16)

    def pick_rows(source, start, width):
        at = pl.ds(pl.multiple_of(start, 128), width)
        return dot(gather, source[:, at]).reshape(EP, MOST, width).astype(BF16)

    send_h[...] = pick_rows(hid, tp * RING, RING)

    def make_picks():
        weight = first * weights[0:1, :] + second * weights[1:2, :]
        weight_hi = weight.astype(BF16)
        weight_lo = (weight - weight_hi.astype(F32)).astype(BF16)
        picks[0:ROWS, :] = jnp.transpose(chosen * dot(spread, weight_hi)).astype(BF16)
        picks[ROWS:, :] = jnp.transpose(chosen * dot(spread, weight_lo)).astype(BF16)

    def remote(src, dst, send, recv, device):
        return pltpu.make_async_remote_copy(
            src_ref=src, dst_ref=dst, send_sem=send, recv_sem=recv, device_id=device, device_id_type=MESH
        )

    def arrived(view, sem):
        remote(view, view, sem, sem, (pod, me, right)).wait_recv()

    def sent(view, sem):
        remote(view, view, sem, sem, (pod, me, right)).wait_send()

    def dispatch(a, send, rows, recv):
        for dz, dx in STEPS:
            peer = expert_at(dz, dx)
            remote(send.at[peer], rows.at[me], disp_s.at[a], recv(dz), (pod, peer, tp)).start()
        pltpu.make_async_copy(send.at[me], rows.at[me], recv(0)).start()

    first_cols, first_cols_g = pl.ds(0, DIRECT), pl.ds(0, DIRECT_G)
    piece_o[:, :, first_cols] = pick_rows(hid, TP * RING, DIRECT)
    pl.semaphore_wait(barrier, len(STEPS) + 4)
    dispatch(0, send_h, rows_h.at[tp], lambda dz: disp_r.at[0, dz])
    for i in range(3):
        remote(
            dense_hbm.at[i], dense_w.at[i, own_rows], core_s.at[i], core_r.at[i], (1 - pod, me, tp)
        ).start()
    dispatch(2, piece_o.at[:, :, first_cols], rows_d, lambda dz: direct_r.at[0])
    send_g[...] = pick_rows(grad, tp * RING_G, RING_G)
    dispatch(1, send_g, rows_g.at[tp], lambda dz: disp_r.at[1, dz])
    if DIRECT_G:
        piece_g[:, :, first_cols_g] = pick_rows(grad, TP * RING_G, DIRECT_G)
        dispatch(3, piece_g.at[:, :, first_cols_g], rows_e, lambda dz: direct_r.at[1])

    def group_of(rows, q, dz):
        at = pl.multiple_of(lax.rem(z - dz + 4, 4) * 4, 4)
        return rows.at[q, pl.ds(at, 4)]

    def ring_out(a, rows, some=(0, 1, 2, 3)):
        for n in some:
            block = group_of(rows, tp, GROUPS[n])
            arrived(block, disp_r.at[a, GROUPS[n]])
            for way, peer in ((0, right), (1, left)):
                remote(block, block, ring_s.at[a], ring_r.at[a, way, n], (pod, me, peer)).start()

    def ring_on(a, rows, way):
        source, peer = ((left, right), (right, left))[way]
        for n in (2 * way, 2 * way + 1):
            block = group_of(rows, source, GROUPS[n])
            arrived(block, ring_r.at[a, way, n])
            remote(block, block, fwd_s.at[a], fwd_r.at[a], (pod, me, peer)).start()

    def ring_in(a, rows, way):
        source = (left, right)[way]
        for n in (2 - 2 * way, 3 - 2 * way):
            arrived(group_of(rows, source, GROUPS[n]), ring_r.at[a, way, n])

    def ring_end(a, rows):
        arrived(rows.at[lax.rem(tp + 2, TP)], fwd_r.at[a])

    def pack(rows, width):
        def step(i, carry):
            block = rows[pl.ds(2 * i, 2)]
            mat_x[pl.ds(pl.multiple_of(i * 2 * MOST, 16), 2 * MOST), 0:width] = (
                block.astype(F32).reshape(2 * MOST, width).astype(BF16)
            )
            return carry

        lax.fori_loop(0, EP // 2, step, 0)

    def forward_part(rows, at, width, start):
        pack(rows, width)
        if start:
            acc_gate[...] = dot(mat_x[:, 0:width], gate_up[0, at, :])
            acc_up[...] = dot(mat_x[:, 0:width], gate_up[1, at, :])
        else:
            acc_gate[...] += dot(mat_x[:, 0:width], gate_up[0, at, :])
            acc_up[...] += dot(mat_x[:, 0:width], gate_up[1, at, :])

    def forward_quarter(q, start):
        at = pl.ds(pl.multiple_of(q * RING, RING), RING)
        forward_part(rows_h.at[q], at, RING, start)

    def backward_part(rows, at, width, start):
        pack(rows, width)
        if start:
            acc_grad[...] = dot(mat_x[:, 0:width], down[at, :])
        else:
            acc_grad[...] += dot(mat_x[:, 0:width], down[at, :])

    def backward_quarter(q, start):
        at = pl.ds(pl.multiple_of(q * RING_G, RING_G), RING_G)
        backward_part(rows_g.at[q], at, RING_G, start)

    def dense_in(i, which):
        at = (own_rows, other_rows)[which]
        left_side = (hid, hid, grad)[i]
        if which == 0:
            dense_loads[i].wait()
            dense_acc[i] = dot(left_side[:, at], dense_w[i, at, :])
        else:
            dense_acc[i] += dot(left_side[:, at], dense_w[i, at, :])

    def dense_landed(i):
        landed = dense_w.at[i, other_rows]
        remote(dense_hbm.at[i], landed, core_s.at[i], core_r.at[i], (1 - pod, me, tp)).wait_recv()

    for i in range(3):
        dense_in(i, 0)
    ring_out(0, rows_h)
    for load in loads:
        load.wait()
    forward_quarter(tp, True)
    dense_landed(0)
    dense_in(0, 1)
    ring_on(0, rows_h, 0)
    dense_landed(1)
    dense_in(1, 1)
    ring_on(0, rows_h, 1)
    ring_in(0, rows_h, 0)
    forward_quarter(left, False)
    ring_in(0, rows_h, 1)
    forward_quarter(right, False)
    arrived(rows_d, direct_r.at[0])
    forward_part(rows_d, pl.ds(TP * RING, DIRECT), DIRECT, False)
    ring_out(1, rows_g, (0, 1))
    ring_end(0, rows_h)
    forward_quarter(lax.rem(tp + 2, TP), False)
    ring_out(1, rows_g, (2, 3))
    peers = pl.ds(0, len(STEPS))
    sent(piece_o.at[peers, :, first_cols], disp_s.at[2])

    silu, slope = silu_parts(acc_gate[...])
    act[0] = (silu * acc_up[...]).astype(BF16)

    def block_at(q):
        return pl.ds(pl.multiple_of(WHOLE_G + q * BLOCK, BLOCK), BLOCK)

    def span(a, c):
        return pl.ds(*((PARTS_O, PARTS_G)[a][c]))

    def send_back(a, c, piece, back):
        cols = span(a, c)
        for dz, dx in STEPS:
            peer = expert_at(dz, dx)
            remote(
                piece.at[peer, :, cols], back.at[me, :, cols], ret_s.at[a, c], ret_r.at[a, c], (pod, peer, tp)
            ).start()
        pltpu.make_async_copy(piece.at[me, :, cols], back.at[me, :, cols], ret_r.at[a, c]).start()

    for c in range(PARTS):
        cols = span(0, c)
        piece_o[:, :, cols] = dot_t(act[0], down[cols, :]).reshape(EP, MOST, cols.size).astype(BF16)
        send_back(0, c, piece_o, back_o)

    dense_landed(2)
    dense_in(2, 1)
    ring_on(1, rows_g, 0)
    d_silu, d_slope = silu_parts(dense_acc[0])
    d_up, d_back = dense_acc[1], dense_acc[2]
    d_act = (d_silu * d_up).astype(BF16)
    d_grad_gate = (d_back * d_up * d_slope).astype(BF16)
    d_grad_up = (d_back * d_silu).astype(BF16)
    for c in range(2):
        half = pl.ds(c * HALF, HALF)
        dense_out[:, half] = dot_t(d_act, dense_w[2, half, :]).astype(BF16)
    ring_on(1, rows_g, 1)
    for c in range(2):
        half = pl.ds(c * HALF, HALF)
        total = dot_t(d_grad_gate, dense_w[0, half, :]) + dot_t(d_grad_up, dense_w[1, half, :])
        dense_grad[:, half] = total.astype(BF16)
    make_picks()
    for d in (2, 1, 3):
        peer = lax.rem(tp + d, TP)
        remote(
            dense_grad.at[:, block_at(peer)], dense_in_x.at[d - 1], dense_s.at[0], dense_r.at[0], (pod, me, peer)
        ).start()
    mine = pl.ds(pl.multiple_of(tp * OWN, OWN), OWN)

    def combine(a, c, back, dense, part, red):
        cols = span(a, c)
        arrived(back.at[:, :, cols], ret_r.at[a, c])
        rows = back[:, :, cols].astype(F32).reshape(SLOTS, cols.size).astype(BF16)
        product = dot(picks[...], rows)
        total = dense[:, cols].astype(F32) + product[:ROWS] + product[ROWS:]
        part[:, cols] = total.astype(BF16)
        for d in (2, 1, 3):
            peer = lax.rem(tp + d, TP)
            rows_at = pl.ds(pl.multiple_of(peer * OWN, OWN), OWN)
            remote(
                part.at[rows_at, cols], red.at[d - 1, :, cols], red_s.at[a, c], red_r.at[a, c], (pod, me, peer)
            ).start()

    def reduced(a, c, part, red):
        cols = span(a, c)
        total = part[mine, cols].astype(F32)
        arrived(red.at[:, :, cols], red_r.at[a, c])
        for d in range(3):
            total = total + red[d, :, cols].astype(F32)
        return total

    def spread_out(k, ref):
        for d in (2, 1, 3):
            remote(ref, ref, gat_s.at[k], gat_r.at[k], (pod, me, lax.rem(tp + d, TP))).start()

    others = pl.ds(0, ROWS - OWN)

    def combine_o(c):
        combine(0, c, back_o, dense_out, part_o, red_o)

    def reduce_o(c):
        cols = span(0, c)
        total = reduced(0, c, part_o, red_o)
        layer_out[mine, cols] = (tok[mine, cols].astype(F32) + total).astype(BF16)
        spread_out(c, layer_out.at[mine, cols])

    backward_quarter(tp, True)
    ring_in(1, rows_g, 0)
    backward_quarter(left, False)
    ring_in(1, rows_g, 1)
    backward_quarter(right, False)
    if DIRECT_G:
        arrived(rows_e, direct_r.at[1])
        backward_part(rows_e, pl.ds(TP * RING_G, DIRECT_G), DIRECT_G, False)
    combine_o(0)
    ring_end(1, rows_g)
    backward_quarter(lax.rem(tp + 2, TP), False)
    if DIRECT_G:
        sent(piece_g.at[peers, :, first_cols_g], disp_s.at[3])
    silu, slope = silu_parts(acc_gate[...])
    act[0] = (acc_grad[...] * acc_up[...] * slope).astype(BF16)
    act[1] = (acc_grad[...] * silu).astype(BF16)

    def grad_piece(cols):
        return dot_t(act[0], gate_up[0, cols, :]) + dot_t(act[1], gate_up[1, cols, :])

    for d in (2, 1, 3):
        peer = lax.rem(tp + d, TP)
        cross_out[d - 1] = grad_piece(block_at(peer)).reshape(EP, MOST, BLOCK).astype(BF16)
        remote(
            cross_out.at[d - 1], cross_in.at[d - 1], cross_s.at[0], cross_r.at[0], (pod, me, peer)
        ).start()
    for c in range(len(PARTS_G)):
        cols = span(1, c)
        piece_g[:, :, cols] = grad_piece(cols).reshape(EP, MOST, cols.size).astype(BF16)
        send_back(1, c, piece_g, back_g)
        if c == 0:
            combine_o(1)
            reduce_o(0)
    merged[...] = grad_piece(block_at(tp)).reshape(EP, MOST, BLOCK).astype(BF16)

    def merge():
        total = merged[...].astype(F32)
        arrived(cross_in, cross_r.at[0])
        for d in range(3):
            total = total + cross_in[d].astype(F32)
        merged[...] = total.astype(BF16)
        for dz, dx in STEPS:
            peer = expert_at(dz, dx)
            remote(merged.at[peer], back_x.at[me], retx_s.at[0], retx_r.at[0], (pod, peer, tp)).start()
        pltpu.make_async_copy(merged.at[me], back_x.at[me], retx_r.at[0]).start()

    def combine_x():
        arrived(back_x, retx_r.at[0])
        rows = back_x[...].astype(F32).reshape(SLOTS, BLOCK).astype(BF16)
        product = dot(picks[...], rows)
        total = dense_grad[:, block_at(tp)].astype(F32) + product[:ROWS] + product[ROWS:]
        arrived(dense_in_x, dense_r.at[0])
        for d in range(3):
            total = total + dense_in_x[d].astype(F32)
        total_g[:, block_at(tp)] = total.astype(BF16)
        spread_out(2 * PARTS - 1, total_g.at[:, block_at(tp)])

    def combine_g(c):
        combine(1, c, back_g, dense_grad, part_g, red_g)

    def reduce_g(c):
        cols = span(1, c)
        total_g[mine, cols] = reduced(1, c, part_g, red_g).astype(BF16)
        spread_out(PARTS + c, total_g.at[mine, cols])

    combine_o(2)
    reduce_o(1)
    combine_o(3)
    merge()
    reduce_o(2)
    reduce_o(3)
    combine_g(0)
    for c in range(1, len(PARTS_G)):
        combine_g(c)
        reduce_g(c - 1)
    combine_x()
    reduce_g(len(PARTS_G) - 1)

    for c in range(PARTS):
        view = layer_out.at[others, span(0, c)]
        arrived(view, gat_r.at[c])
        sent(view, gat_s.at[c])
        sent(red_o.at[:, :, span(0, c)], red_s.at[0, c])
        sent(piece_o.at[peers, :, span(0, c)], ret_s.at[0, c])
    for c in range(len(PARTS_G)):
        view = total_g.at[others, span(1, c)]
        arrived(view, gat_r.at[PARTS + c])
        sent(view, gat_s.at[PARTS + c])
        sent(red_g.at[:, :, span(1, c)], red_s.at[1, c])
        sent(piece_g.at[peers, :, span(1, c)], ret_s.at[1, c])
    arrived(dense_in_x, gat_r.at[2 * PARTS - 1])
    sent(dense_in_x, gat_s.at[2 * PARTS - 1])
    sent(dense_in_x, dense_s.at[0])
    sent(cross_out, cross_s.at[0])
    sent(merged.at[peers], retx_s.at[0])
    for i in range(3):
        sent(dense_hbm.at[i], core_s.at[i])
    for a, send, rows in ((0, send_h, rows_h), (1, send_g, rows_g)):
        sent(send.at[peers], disp_s.at[a])
        sent(rows.at[pl.ds(0, 2)], ring_s.at[a])
        sent(rows.at[0], fwd_s.at[a])


def finish(tok, gain, grad, total_g, layer_in, layer_out, grad_in):
    layer_out[...] = layer_in[...]
    float_in = tok[...].astype(F32)
    inverse = lax.rsqrt(jnp.mean(float_in * float_in, axis=1, keepdims=True) + EPS)
    normed = float_in * inverse
    scaled = total_g[...].astype(F32) * gain[...].reshape(1, D)
    project = jnp.mean(scaled * normed, axis=1, keepdims=True)
    grad_in[...] = (grad[...].astype(F32) + inverse * (scaled - normed * project)).astype(BF16)


def body(tokens, norm_gain, dense_weight, expert_gate_up, expert_down, expert_ids, gate_weights, grad_out):
    vmem = pl.BlockSpec(memory_space=pltpu.VMEM)
    hbm = pl.BlockSpec(memory_space=pl.ANY)
    dma = pltpu.SemaphoreType.DMA
    steps = len(STEPS)
    row_shape = jax.ShapeDtypeStruct((ROWS, D), BF16)
    layer_sum, grad_sum = pl.pallas_call(
        kernel,
        name="layer",
        out_shape=[row_shape, row_shape],
        in_specs=[vmem, vmem, hbm, hbm, hbm, vmem, vmem, vmem],
        out_specs=[vmem, vmem],
        scratch_shapes=[
            pltpu.VMEM((3, D, FF), BF16),
            pltpu.VMEM((2, D, FF), BF16),
            pltpu.VMEM((D, FF), BF16),
            pltpu.VMEM((ROWS, D), BF16),
            pltpu.VMEM((EP, MOST, RING), BF16),
            pltpu.VMEM((EP, MOST, RING_G), BF16),
            pltpu.VMEM((TP, EP, MOST, RING), BF16),
            pltpu.VMEM((EP, MOST, DIRECT), BF16),
            pltpu.VMEM((TP, EP, MOST, RING_G), BF16),
            pltpu.VMEM((EP, MOST, max(DIRECT_G, 128)), BF16),
            pltpu.VMEM((SLOTS, max(DIRECT, RING_G)), BF16),
            pltpu.VMEM((SLOTS, FF), F32),
            pltpu.VMEM((SLOTS, FF), F32),
            pltpu.VMEM((SLOTS, FF), F32),
            pltpu.VMEM((2, SLOTS, FF), BF16),
            pltpu.VMEM((ROWS, D), BF16),
            pltpu.VMEM((ROWS, D), BF16),
            pltpu.VMEM((EP, MOST, D), BF16),
            pltpu.VMEM((EP, MOST, WHOLE_G), BF16),
            pltpu.VMEM((EP, MOST, D), BF16),
            pltpu.VMEM((EP, MOST, WHOLE_G), BF16),
            pltpu.VMEM((ROWS, D), BF16),
            pltpu.VMEM((ROWS, WHOLE_G), BF16),
            pltpu.VMEM((3, OWN, D), BF16),
            pltpu.VMEM((3, OWN, WHOLE_G), BF16),
            pltpu.VMEM((2 * ROWS, SLOTS), BF16),
            pltpu.VMEM((3, ROWS, FF), F32),
            pltpu.VMEM((3, EP, MOST, BLOCK), BF16),
            pltpu.VMEM((3, EP, MOST, BLOCK), BF16),
            pltpu.VMEM((EP, MOST, BLOCK), BF16),
            pltpu.VMEM((EP, MOST, BLOCK), BF16),
            pltpu.VMEM((3, ROWS, BLOCK), BF16),
            dma((5,)),
            dma((3,)),
            dma((3,)),
            dma((4,)),
            dma((2,)),
            dma((2, 2, 4)),
            dma((2,)),
            dma((2,)),
            dma((2, 4)),
            dma((2,)),
            dma((2, PARTS)),
            dma((2, PARTS)),
            dma((2, PARTS)),
            dma((2, PARTS)),
            dma((2 * PARTS,)),
            dma((2 * PARTS,)),
            dma((1,)),
            dma((1,)),
            dma((1,)),
            dma((1,)),
            dma((1,)),
            dma((1,)),
        ],
        compiler_params=pltpu.CompilerParams(
            collective_id=0, has_side_effects=True, vmem_limit_bytes=63 * 2**20
        ),
    )(
        tokens, norm_gain, dense_weight, expert_gate_up, expert_down,
        expert_ids.T, gate_weights.T, grad_out,
    )
    block = pl.BlockSpec((ROWS // 2, D), lambda i: (i, 0))
    return pl.pallas_call(
        finish,
        name="finish",
        grid=(2,),
        out_shape=[row_shape, row_shape],
        in_specs=[block, pl.BlockSpec((D,), lambda i: (0,)), block, block, block],
        out_specs=[block, block],
    )(tokens, norm_gain, grad_out, grad_sum, layer_sum)


def solution(mesh):
    rows = P(("outer", "ep"), None)
    in_specs = (rows, P(), P(None, "outer", "tp"), P("ep", None, None, "tp"), P("ep", None, "tp"), rows, rows, rows)
    return jax.shard_map(body, mesh=mesh, in_specs=in_specs, out_specs=(rows, rows), check_vma=False)
```

```python
import jax
import jax.numpy as jnp
from jax import lax
from jax.experimental import pallas as pl
from jax.experimental.pallas import tpu as pltpu
from jax.sharding import PartitionSpec as P

MESH = pl.DeviceIdType.MESH
F32 = jnp.float32
BF16 = jnp.bfloat16
ROWS = 128
D = 3584
FF = 640
EP = 16
TP = 4
MOST = 24
SLOTS = EP * MOST
RING = 640
DIRECT = D - TP * RING
RING_G = 768
DIRECT_G = D - TP * RING_G
HALF = D // 2
PARTS_O = ((0, 896), (896, 896), (1792, 896), (2688, 896))
BLOCK = 256
WHOLE_G = D - TP * BLOCK
PARTS_G = ((0, 768), (768, 768), (1536, 640), (2176, WHOLE_G - 2176))
PARTS = 5
OWN = ROWS // TP
EPS = 1e-05
STEPS = [(dz, dx) for dz in (0, 1, 3, 2) for dx in range(4) if (dz, dx) != (0, 0)]
GROUPS = (0, 1, 3, 2)


def silu_parts(values):
    sigmoid_v = jax.nn.sigmoid(values)
    return (values * sigmoid_v, sigmoid_v * (1.0 + values * (1.0 - sigmoid_v)))


def dot(left, right):
    return jnp.dot(left, right, preferred_element_type=F32)


def dot_t(left, right):
    return lax.dot_general(left, right, (((1,), (1,)), ((), ())), preferred_element_type=F32)


def kernel(
    tok_hbm, gain, dense_hbm, gate_up_hbm, down_hbm, ids, weights, grad_hbm,
    layer_out, total_g,
    tok, grad, dense_w, gate_up, down, hid, send_h, send_g, rows_h, rows_d, rows_g, rows_e, mat_x,
    acc_gate, acc_up, acc_grad, act, dense_out, dense_grad,
    piece_o, piece_g, back_o, back_g, part_o, part_g, red_o, red_g,
    picks, dense_acc, cross_out, cross_in, merged, back_x, dense_in_x,
    load_sem, core_s, core_r, disp_s, ring_s, ring_r, fwd_s, fwd_r, disp_r, direct_r,
    ret_s, ret_r, red_s, red_r, gat_s, gat_r,
    cross_s, cross_r, dense_s, dense_r, retx_s, retx_r,
):
    pod, me, tp = lax.axis_index("outer"), lax.axis_index("ep"), lax.axis_index("tp")
    z, x = me // 4, lax.rem(me, 4)
    right, left = lax.rem(tp + 1, TP), lax.rem(tp + 3, TP)

    def expert_at(dz, dx):
        return lax.rem(z + dz + 4, 4) * 4 + lax.rem(x + dx + 4, 4)

    barrier = pltpu.get_barrier_semaphore()
    for dz, dx in STEPS:
        pl.semaphore_signal(barrier, inc=1, device_id=(pod, expert_at(dz, dx), tp), device_id_type=MESH)
    for d in (1, 2, 3):
        pl.semaphore_signal(barrier, inc=1, device_id=(pod, me, lax.rem(tp + d, TP)), device_id_type=MESH)
    pl.semaphore_signal(barrier, inc=1, device_id=(1 - pod, me, tp), device_id_type=MESH)

    row_loads = [
        pltpu.make_async_copy(tok_hbm, tok, load_sem.at[5]),
        pltpu.make_async_copy(grad_hbm, grad, load_sem.at[6]),
    ]
    loads = [
        pltpu.make_async_copy(gate_up_hbm.at[0], gate_up, load_sem.at[0]),
        pltpu.make_async_copy(down_hbm.at[0], down, load_sem.at[1]),
    ]
    own_rows = pl.ds(pl.multiple_of(pod * HALF, HALF), HALF)
    other_rows = pl.ds(pl.multiple_of((1 - pod) * HALF, HALF), HALF)
    dense_loads = [
        pltpu.make_async_copy(dense_hbm.at[i], dense_w.at[i, own_rows], load_sem.at[2 + i])
        for i in range(3)
    ]
    for load in row_loads + loads + dense_loads:
        load.start()
    row_loads[0].wait()

    float_in = tok[...].astype(F32)
    inverse = lax.rsqrt(jnp.mean(float_in * float_in, axis=1, keepdims=True) + EPS)
    hid[...] = (float_in * inverse * gain[...].reshape(1, D)).astype(BF16)

    experts = lax.broadcasted_iota(jnp.int32, (EP, ROWS), 0)
    first = (ids[0:1, :] == experts).astype(F32)
    second = (ids[1:2, :] == experts).astype(F32)
    named = (first + second).astype(BF16)
    before = (
        lax.broadcasted_iota(jnp.int32, (ROWS, ROWS), 0)
        < lax.broadcasted_iota(jnp.int32, (ROWS, ROWS), 1)
    ).astype(F32).astype(BF16)
    rank = dot(named, before)
    slot = lax.broadcasted_iota(jnp.int32, (SLOTS, EP), 0)
    low = lax.broadcasted_iota(jnp.int32, (SLOTS, EP), 1) * MOST
    spread = ((slot >= low) & (slot < low + MOST)).astype(F32).astype(BF16)
    slot_f = lax.broadcasted_iota(jnp.int32, (SLOTS, ROWS), 0).astype(F32)
    within = slot_f - MOST * jnp.floor((slot_f + 0.5) * (1.0 / MOST))
    named_at = dot(spread, named)
    rank_at = dot(spread, rank.astype(BF16))
    chosen = jnp.where((named_at > 0.5) & (jnp.abs(rank_at - within) < 0.5), 1.0, 0.0)
    gather = chosen.astype(BF16)

    def pick_rows(source, start, width):
        at = pl.ds(pl.multiple_of(start, 128), width)
        return dot(gather, source[:, at]).reshape(EP, MOST, width).astype(BF16)

    send_h[...] = pick_rows(hid, tp * RING, RING)

    def make_picks():
        weight = first * weights[0:1, :] + second * weights[1:2, :]
        weight_hi = weight.astype(BF16)
        weight_lo = (weight - weight_hi.astype(F32)).astype(BF16)
        picks[0:ROWS, :] = jnp.transpose(chosen * dot(spread, weight_hi)).astype(BF16)
        picks[ROWS:, :] = jnp.transpose(chosen * dot(spread, weight_lo)).astype(BF16)

    def remote(src, dst, send, recv, device):
        return pltpu.make_async_remote_copy(
            src_ref=src, dst_ref=dst, send_sem=send, recv_sem=recv, device_id=device, device_id_type=MESH
        )

    def arrived(view, sem):
        remote(view, view, sem, sem, (pod, me, right)).wait_recv()

    def sent(view, sem):
        remote(view, view, sem, sem, (pod, me, right)).wait_send()

    def dispatch(a, send, rows, recv):
        for dz, dx in STEPS:
            peer = expert_at(dz, dx)
            remote(send.at[peer], rows.at[me], disp_s.at[a], recv(dz), (pod, peer, tp)).start()
        pltpu.make_async_copy(send.at[me], rows.at[me], recv(0)).start()

    first_cols, first_cols_g = pl.ds(0, DIRECT), pl.ds(0, DIRECT_G)
    piece_o[:, :, first_cols] = pick_rows(hid, TP * RING, DIRECT)
    pl.semaphore_wait(barrier, len(STEPS) + 4)
    dispatch(0, send_h, rows_h.at[tp], lambda dz: disp_r.at[0, dz])
    for i in range(3):
        remote(
            dense_hbm.at[i], dense_w.at[i, own_rows], core_s.at[i], core_r.at[i], (1 - pod, me, tp)
        ).start()
    dispatch(2, piece_o.at[:, :, first_cols], rows_d, lambda dz: direct_r.at[0])
    row_loads[1].wait()
    send_g[...] = pick_rows(grad, tp * RING_G, RING_G)
    dispatch(1, send_g, rows_g.at[tp], lambda dz: disp_r.at[1, dz])
    if DIRECT_G:
        piece_g[:, :, first_cols_g] = pick_rows(grad, TP * RING_G, DIRECT_G)
        dispatch(3, piece_g.at[:, :, first_cols_g], rows_e, lambda dz: direct_r.at[1])

    def group_of(rows, q, dz):
        at = pl.multiple_of(lax.rem(z - dz + 4, 4) * 4, 4)
        return rows.at[q, pl.ds(at, 4)]

    def ring_out(a, rows, some=(0, 1, 2, 3)):
        for n in some:
            block = group_of(rows, tp, GROUPS[n])
            arrived(block, disp_r.at[a, GROUPS[n]])
            for way, peer in ((0, right), (1, left)):
                remote(block, block, ring_s.at[a], ring_r.at[a, way, n], (pod, me, peer)).start()

    def ring_on(a, rows, way):
        source, peer = ((left, right), (right, left))[way]
        for n in (2 * way, 2 * way + 1):
            block = group_of(rows, source, GROUPS[n])
            arrived(block, ring_r.at[a, way, n])
            remote(block, block, fwd_s.at[a], fwd_r.at[a], (pod, me, peer)).start()

    def ring_in(a, rows, way):
        source = (left, right)[way]
        for n in (2 - 2 * way, 3 - 2 * way):
            arrived(group_of(rows, source, GROUPS[n]), ring_r.at[a, way, n])

    def ring_end(a, rows):
        arrived(rows.at[lax.rem(tp + 2, TP)], fwd_r.at[a])

    def pack(rows, width):
        def step(i, carry):
            block = rows[pl.ds(2 * i, 2)]
            mat_x[pl.ds(pl.multiple_of(i * 2 * MOST, 16), 2 * MOST), 0:width] = (
                block.astype(F32).reshape(2 * MOST, width).astype(BF16)
            )
            return carry

        lax.fori_loop(0, EP // 2, step, 0)

    def forward_part(rows, at, width, start):
        pack(rows, width)
        if start:
            acc_gate[...] = dot(mat_x[:, 0:width], gate_up[0, at, :])
            acc_up[...] = dot(mat_x[:, 0:width], gate_up[1, at, :])
        else:
            acc_gate[...] += dot(mat_x[:, 0:width], gate_up[0, at, :])
            acc_up[...] += dot(mat_x[:, 0:width], gate_up[1, at, :])

    def forward_quarter(q, start):
        at = pl.ds(pl.multiple_of(q * RING, RING), RING)
        forward_part(rows_h.at[q], at, RING, start)

    def backward_part(rows, at, width, start):
        pack(rows, width)
        if start:
            acc_grad[...] = dot(mat_x[:, 0:width], down[at, :])
        else:
            acc_grad[...] += dot(mat_x[:, 0:width], down[at, :])

    def backward_quarter(q, start):
        at = pl.ds(pl.multiple_of(q * RING_G, RING_G), RING_G)
        backward_part(rows_g.at[q], at, RING_G, start)

    def dense_in(i, which):
        at = (own_rows, other_rows)[which]
        left_side = (hid, hid, grad)[i]
        if which == 0:
            dense_loads[i].wait()
            dense_acc[i] = dot(left_side[:, at], dense_w[i, at, :])
        else:
            dense_acc[i] += dot(left_side[:, at], dense_w[i, at, :])

    def dense_landed(i):
        landed = dense_w.at[i, other_rows]
        remote(dense_hbm.at[i], landed, core_s.at[i], core_r.at[i], (1 - pod, me, tp)).wait_recv()

    for i in range(3):
        dense_in(i, 0)
    ring_out(0, rows_h)
    for load in loads:
        load.wait()
    forward_quarter(tp, True)
    dense_landed(0)
    dense_in(0, 1)
    ring_on(0, rows_h, 0)
    dense_landed(1)
    dense_in(1, 1)
    ring_on(0, rows_h, 1)
    ring_in(0, rows_h, 0)
    forward_quarter(left, False)
    ring_in(0, rows_h, 1)
    forward_quarter(right, False)
    arrived(rows_d, direct_r.at[0])
    forward_part(rows_d, pl.ds(TP * RING, DIRECT), DIRECT, False)
    ring_out(1, rows_g, (0, 1))
    ring_end(0, rows_h)
    forward_quarter(lax.rem(tp + 2, TP), False)
    ring_out(1, rows_g, (2, 3))
    peers = pl.ds(0, len(STEPS))
    sent(piece_o.at[peers, :, first_cols], disp_s.at[2])

    silu, slope = silu_parts(acc_gate[...])
    act[0] = (silu * acc_up[...]).astype(BF16)

    def block_at(q):
        return pl.ds(pl.multiple_of(WHOLE_G + q * BLOCK, BLOCK), BLOCK)

    def span(a, c):
        return pl.ds(*((PARTS_O, PARTS_G)[a][c]))

    def send_back(a, c, piece, back):
        cols = span(a, c)
        for dz, dx in STEPS:
            peer = expert_at(dz, dx)
            remote(
                piece.at[peer, :, cols], back.at[me, :, cols], ret_s.at[a, c], ret_r.at[a, c], (pod, peer, tp)
            ).start()
        pltpu.make_async_copy(piece.at[me, :, cols], back.at[me, :, cols], ret_r.at[a, c]).start()

    for c in range(4):
        cols = span(0, c)
        piece_o[:, :, cols] = dot_t(act[0], down[cols, :]).reshape(EP, MOST, cols.size).astype(BF16)
        send_back(0, c, piece_o, back_o)

    dense_landed(2)
    dense_in(2, 1)
    ring_on(1, rows_g, 0)
    d_silu, d_slope = silu_parts(dense_acc[0])
    d_up, d_back = dense_acc[1], dense_acc[2]
    d_act = (d_silu * d_up).astype(BF16)
    d_grad_gate = (d_back * d_up * d_slope).astype(BF16)
    d_grad_up = (d_back * d_silu).astype(BF16)
    for c in range(2):
        half = pl.ds(c * HALF, HALF)
        dense_out[:, half] = dot_t(d_act, dense_w[2, half, :]).astype(BF16)
    ring_on(1, rows_g, 1)
    for c in range(2):
        half = pl.ds(c * HALF, HALF)
        total = dot_t(d_grad_gate, dense_w[0, half, :]) + dot_t(d_grad_up, dense_w[1, half, :])
        dense_grad[:, half] = total.astype(BF16)
    make_picks()
    for d in (2, 1, 3):
        peer = lax.rem(tp + d, TP)
        remote(
            dense_grad.at[:, block_at(peer)], dense_in_x.at[d - 1], dense_s.at[0], dense_r.at[0], (pod, me, peer)
        ).start()
    mine = pl.ds(pl.multiple_of(tp * OWN, OWN), OWN)

    def combine(a, c, back, dense, part, red):
        cols = span(a, c)
        arrived(back.at[:, :, cols], ret_r.at[a, c])
        rows = back[:, :, cols].astype(F32).reshape(SLOTS, cols.size).astype(BF16)
        product = dot(picks[...], rows)
        total = dense[:, cols].astype(F32) + product[:ROWS] + product[ROWS:]
        part[:, cols] = total.astype(BF16)
        for d in (2, 1, 3):
            peer = lax.rem(tp + d, TP)
            rows_at = pl.ds(pl.multiple_of(peer * OWN, OWN), OWN)
            remote(
                part.at[rows_at, cols], red.at[d - 1, :, cols], red_s.at[a, c], red_r.at[a, c], (pod, me, peer)
            ).start()

    def reduced(a, c, part, red):
        cols = span(a, c)
        total = part[mine, cols].astype(F32)
        arrived(red.at[:, :, cols], red_r.at[a, c])
        for d in range(3):
            total = total + red[d, :, cols].astype(F32)
        return total

    def spread_out(k, ref, target):
        for d in (2, 1, 3):
            remote(ref, target, gat_s.at[k], gat_r.at[k], (pod, me, lax.rem(tp + d, TP))).start()
        pltpu.make_async_copy(ref, target, gat_r.at[k]).start()

    others = pl.ds(0, ROWS - OWN)

    def combine_o(c):
        combine(0, c, back_o, dense_out, part_o, red_o)

    def reduce_o(c):
        cols = span(0, c)
        total = reduced(0, c, part_o, red_o)
        part_o[mine, cols] = (tok[mine, cols].astype(F32) + total).astype(BF16)
        spread_out(c, part_o.at[mine, cols], layer_out.at[mine, cols])

    backward_quarter(tp, True)
    ring_in(1, rows_g, 0)
    backward_quarter(left, False)
    ring_in(1, rows_g, 1)
    backward_quarter(right, False)
    if DIRECT_G:
        arrived(rows_e, direct_r.at[1])
        backward_part(rows_e, pl.ds(TP * RING_G, DIRECT_G), DIRECT_G, False)
    combine_o(0)
    ring_end(1, rows_g)
    backward_quarter(lax.rem(tp + 2, TP), False)
    if DIRECT_G:
        sent(piece_g.at[peers, :, first_cols_g], disp_s.at[3])
    silu, slope = silu_parts(acc_gate[...])
    act[0] = (acc_grad[...] * acc_up[...] * slope).astype(BF16)
    act[1] = (acc_grad[...] * silu).astype(BF16)

    def grad_piece(cols):
        return dot_t(act[0], gate_up[0, cols, :]) + dot_t(act[1], gate_up[1, cols, :])

    for d in (2, 1, 3):
        peer = lax.rem(tp + d, TP)
        cross_out[d - 1] = grad_piece(block_at(peer)).reshape(EP, MOST, BLOCK).astype(BF16)
        remote(
            cross_out.at[d - 1], cross_in.at[d - 1], cross_s.at[0], cross_r.at[0], (pod, me, peer)
        ).start()
    for c in range(len(PARTS_G)):
        cols = span(1, c)
        piece_g[:, :, cols] = grad_piece(cols).reshape(EP, MOST, cols.size).astype(BF16)
        send_back(1, c, piece_g, back_g)
        if c == 0:
            combine_o(1)
            reduce_o(0)
    merged[...] = grad_piece(block_at(tp)).reshape(EP, MOST, BLOCK).astype(BF16)

    def merge():
        total = merged[...].astype(F32)
        arrived(cross_in, cross_r.at[0])
        for d in range(3):
            total = total + cross_in[d].astype(F32)
        merged[...] = total.astype(BF16)
        for dz, dx in STEPS:
            peer = expert_at(dz, dx)
            remote(merged.at[peer], back_x.at[me], retx_s.at[0], retx_r.at[0], (pod, peer, tp)).start()
        pltpu.make_async_copy(merged.at[me], back_x.at[me], retx_r.at[0]).start()

    def combine_x():
        arrived(back_x, retx_r.at[0])
        rows = back_x[...].astype(F32).reshape(SLOTS, BLOCK).astype(BF16)
        product = dot(picks[...], rows)
        total = dense_grad[:, block_at(tp)].astype(F32) + product[:ROWS] + product[ROWS:]
        arrived(dense_in_x, dense_r.at[0])
        for d in range(3):
            total = total + dense_in_x[d].astype(F32)
        dense_in_x[0] = total.astype(BF16)
        spread_out(2 * PARTS - 1, dense_in_x.at[0], total_g.at[:, block_at(tp)])

    def combine_g(c):
        combine(1, c, back_g, dense_grad, part_g, red_g)

    def reduce_g(c):
        cols = span(1, c)
        part_g[mine, cols] = reduced(1, c, part_g, red_g).astype(BF16)
        spread_out(PARTS + c, part_g.at[mine, cols], total_g.at[mine, cols])

    combine_o(2)
    reduce_o(1)
    combine_o(3)
    merge()
    reduce_o(2)
    reduce_o(3)
    combine_g(0)
    for c in range(1, len(PARTS_G)):
        combine_g(c)
        reduce_g(c - 1)
    combine_x()
    reduce_g(len(PARTS_G) - 1)

    for c in range(4):
        arrived(layer_out.at[:, span(0, c)], gat_r.at[c])
        sent(part_o.at[others, span(0, c)], gat_s.at[c])
        sent(red_o.at[:, :, span(0, c)], red_s.at[0, c])
        sent(piece_o.at[peers, :, span(0, c)], ret_s.at[0, c])
    for c in range(len(PARTS_G)):
        arrived(total_g.at[:, span(1, c)], gat_r.at[PARTS + c])
        sent(part_g.at[others, span(1, c)], gat_s.at[PARTS + c])
        sent(red_g.at[:, :, span(1, c)], red_s.at[1, c])
        sent(piece_g.at[peers, :, span(1, c)], ret_s.at[1, c])
    arrived(total_g.at[:, pl.ds(WHOLE_G, TP * BLOCK)], gat_r.at[2 * PARTS - 1])
    sent(dense_in_x, gat_s.at[2 * PARTS - 1])
    sent(dense_in_x, dense_s.at[0])
    sent(cross_out, cross_s.at[0])
    sent(merged.at[peers], retx_s.at[0])
    for i in range(3):
        sent(dense_hbm.at[i], core_s.at[i])
    for a, send, rows in ((0, send_h, rows_h), (1, send_g, rows_g)):
        sent(send.at[peers], disp_s.at[a])
        sent(rows.at[pl.ds(0, 2)], ring_s.at[a])
        sent(rows.at[0], fwd_s.at[a])


def finish(tok, gain, grad, total_g, layer_in, layer_out, grad_in):
    layer_out[...] = layer_in[...]
    float_in = tok[...].astype(F32)
    inverse = lax.rsqrt(jnp.mean(float_in * float_in, axis=1, keepdims=True) + EPS)
    normed = float_in * inverse
    scaled = total_g[...].astype(F32) * gain[...].reshape(1, D)
    project = jnp.mean(scaled * normed, axis=1, keepdims=True)
    grad_in[...] = (grad[...].astype(F32) + inverse * (scaled - normed * project)).astype(BF16)


def body(tokens, norm_gain, dense_weight, expert_gate_up, expert_down, expert_ids, gate_weights, grad_out):
    vmem = pl.BlockSpec(memory_space=pltpu.VMEM)
    hbm = pl.BlockSpec(memory_space=pl.ANY)
    dma = pltpu.SemaphoreType.DMA
    steps = len(STEPS)
    row_shape = jax.ShapeDtypeStruct((ROWS, D), BF16)
    layer_sum, grad_sum = pl.pallas_call(
        kernel,
        name="layer",
        out_shape=[row_shape, row_shape],
        in_specs=[hbm, vmem, hbm, hbm, hbm, vmem, vmem, hbm],
        out_specs=[hbm, hbm],
        scratch_shapes=[
            pltpu.VMEM((ROWS, D), BF16),
            pltpu.VMEM((ROWS, D), BF16),
            pltpu.VMEM((3, D, FF), BF16),
            pltpu.VMEM((2, D, FF), BF16),
            pltpu.VMEM((D, FF), BF16),
            pltpu.VMEM((ROWS, D), BF16),
            pltpu.VMEM((EP, MOST, RING), BF16),
            pltpu.VMEM((EP, MOST, RING_G), BF16),
            pltpu.VMEM((TP, EP, MOST, RING), BF16),
            pltpu.VMEM((EP, MOST, DIRECT), BF16),
            pltpu.VMEM((TP, EP, MOST, RING_G), BF16),
            pltpu.VMEM((EP, MOST, max(DIRECT_G, 128)), BF16),
            pltpu.VMEM((SLOTS, max(DIRECT, RING_G)), BF16),
            pltpu.VMEM((SLOTS, FF), F32),
            pltpu.VMEM((SLOTS, FF), F32),
            pltpu.VMEM((SLOTS, FF), F32),
            pltpu.VMEM((2, SLOTS, FF), BF16),
            pltpu.VMEM((ROWS, D), BF16),
            pltpu.VMEM((ROWS, D), BF16),
            pltpu.VMEM((EP, MOST, D), BF16),
            pltpu.VMEM((EP, MOST, WHOLE_G), BF16),
            pltpu.VMEM((EP, MOST, D), BF16),
            pltpu.VMEM((EP, MOST, WHOLE_G), BF16),
            pltpu.VMEM((ROWS, D), BF16),
            pltpu.VMEM((ROWS, WHOLE_G), BF16),
            pltpu.VMEM((3, OWN, D), BF16),
            pltpu.VMEM((3, OWN, WHOLE_G), BF16),
            pltpu.VMEM((2 * ROWS, SLOTS), BF16),
            pltpu.VMEM((3, ROWS, FF), F32),
            pltpu.VMEM((3, EP, MOST, BLOCK), BF16),
            pltpu.VMEM((3, EP, MOST, BLOCK), BF16),
            pltpu.VMEM((EP, MOST, BLOCK), BF16),
            pltpu.VMEM((EP, MOST, BLOCK), BF16),
            pltpu.VMEM((3, ROWS, BLOCK), BF16),
            dma((7,)),
            dma((3,)),
            dma((3,)),
            dma((4,)),
            dma((2,)),
            dma((2, 2, 4)),
            dma((2,)),
            dma((2,)),
            dma((2, 4)),
            dma((2,)),
            dma((2, PARTS)),
            dma((2, PARTS)),
            dma((2, PARTS)),
            dma((2, PARTS)),
            dma((2 * PARTS,)),
            dma((2 * PARTS,)),
            dma((1,)),
            dma((1,)),
            dma((1,)),
            dma((1,)),
            dma((1,)),
            dma((1,)),
        ],
        compiler_params=pltpu.CompilerParams(
            collective_id=0, has_side_effects=True, vmem_limit_bytes=63 * 2**20
        ),
    )(
        tokens, norm_gain, dense_weight, expert_gate_up, expert_down,
        expert_ids.T, gate_weights.T, grad_out,
    )
    block = pl.BlockSpec((ROWS // 2, D), lambda i: (i, 0))
    return pl.pallas_call(
        finish,
        name="finish",
        grid=(2,),
        out_shape=[row_shape, row_shape],
        in_specs=[block, pl.BlockSpec((D,), lambda i: (0,)), block, block, block],
        out_specs=[block, block],
    )(tokens, norm_gain, grad_out, grad_sum, layer_sum)


def solution(mesh):
    rows = P(("outer", "ep"), None)
    in_specs = (rows, P(), P(None, "outer", "tp"), P("ep", None, None, "tp"), P("ep", None, "tp"), rows, rows, rows)
    return jax.shard_map(body, mesh=mesh, in_specs=in_specs, out_specs=(rows, rows), check_vma=False)
```

```python
import jax
import jax.numpy as jnp
from jax import lax
from jax.experimental import pallas as pl
from jax.experimental.pallas import tpu as pltpu
from jax.sharding import PartitionSpec as P

MESH = pl.DeviceIdType.MESH
F32 = jnp.float32
BF16 = jnp.bfloat16
ROWS = 128
D = 3584
FF = 640
EP = 16
TP = 4
MOST = 24
SLOTS = EP * MOST
RING = 640
DIRECT = D - TP * RING
RING_G = 768
DIRECT_G = D - TP * RING_G
HALF = D // 2
PARTS_O = ((0, 640), (640, 1024), (1664, 1024), (2688, 896))
BLOCK = 256
WHOLE_G = D - TP * BLOCK
PARTS_G = ((0, 768), (768, 768), (1536, 640), (2176, WHOLE_G - 2176))
PARTS = 5
OWN = ROWS // TP
EPS = 1e-05
STEPS = [(dz, dx) for dz in (0, 1, 3, 2) for dx in range(4) if (dz, dx) != (0, 0)]
GROUPS = (0, 1, 3, 2)


def silu_parts(values):
    sigmoid_v = jax.nn.sigmoid(values)
    return (values * sigmoid_v, sigmoid_v * (1.0 + values * (1.0 - sigmoid_v)))


def dot(left, right):
    return jnp.dot(left, right, preferred_element_type=F32)


def dot_t(left, right):
    return lax.dot_general(left, right, (((1,), (1,)), ((), ())), preferred_element_type=F32)


def kernel(
    tok_hbm, gain, dense_hbm, gate_up_hbm, down_hbm, ids, weights, grad_hbm,
    layer_out, total_g,
    tok, grad, dense_w, gate_up, down, hid, send_h, send_g, rows_h, rows_d, rows_g, rows_e, mat_x,
    acc_gate, acc_up, acc_grad, act, dense_out, dense_grad,
    piece_o, piece_g, back_o, back_g, part_o, part_g, red_o, red_g,
    picks, dense_acc, cross_out, cross_in, merged, back_x, dense_in_x,
    load_sem, core_s, core_r, disp_s, ring_s, ring_r, fwd_s, fwd_r, disp_r, direct_r,
    ret_s, ret_r, red_s, red_r, gat_s, gat_r,
    cross_s, cross_r, dense_s, dense_r, retx_s, retx_r,
):
    pod, me, tp = lax.axis_index("outer"), lax.axis_index("ep"), lax.axis_index("tp")
    z, x = me // 4, lax.rem(me, 4)
    right, left = lax.rem(tp + 1, TP), lax.rem(tp + 3, TP)

    def expert_at(dz, dx):
        return lax.rem(z + dz + 4, 4) * 4 + lax.rem(x + dx + 4, 4)

    barrier = pltpu.get_barrier_semaphore()
    for dz, dx in STEPS:
        pl.semaphore_signal(barrier, inc=1, device_id=(pod, expert_at(dz, dx), tp), device_id_type=MESH)
    for d in (1, 2, 3):
        pl.semaphore_signal(barrier, inc=1, device_id=(pod, me, lax.rem(tp + d, TP)), device_id_type=MESH)
    pl.semaphore_signal(barrier, inc=1, device_id=(1 - pod, me, tp), device_id_type=MESH)

    row_loads = [
        pltpu.make_async_copy(tok_hbm, tok, load_sem.at[5]),
        pltpu.make_async_copy(grad_hbm, grad, load_sem.at[6]),
    ]
    loads = [
        pltpu.make_async_copy(gate_up_hbm.at[0], gate_up, load_sem.at[0]),
        pltpu.make_async_copy(down_hbm.at[0], down, load_sem.at[1]),
    ]
    own_rows = pl.ds(pl.multiple_of(pod * HALF, HALF), HALF)
    other_rows = pl.ds(pl.multiple_of((1 - pod) * HALF, HALF), HALF)
    dense_loads = [
        pltpu.make_async_copy(dense_hbm.at[i], dense_w.at[i, own_rows], load_sem.at[2 + i])
        for i in range(3)
    ]
    for load in row_loads + loads + dense_loads:
        load.start()
    row_loads[0].wait()

    float_in = tok[...].astype(F32)
    inverse = lax.rsqrt(jnp.mean(float_in * float_in, axis=1, keepdims=True) + EPS)
    hid[...] = (float_in * inverse * gain[...].reshape(1, D)).astype(BF16)

    experts = lax.broadcasted_iota(jnp.int32, (EP, ROWS), 0)
    first = (ids[0:1, :] == experts).astype(F32)
    second = (ids[1:2, :] == experts).astype(F32)
    named = (first + second).astype(BF16)
    before = (
        lax.broadcasted_iota(jnp.int32, (ROWS, ROWS), 0)
        < lax.broadcasted_iota(jnp.int32, (ROWS, ROWS), 1)
    ).astype(F32).astype(BF16)
    rank = dot(named, before)
    slot = lax.broadcasted_iota(jnp.int32, (SLOTS, EP), 0)
    low = lax.broadcasted_iota(jnp.int32, (SLOTS, EP), 1) * MOST
    spread = ((slot >= low) & (slot < low + MOST)).astype(F32).astype(BF16)
    slot_f = lax.broadcasted_iota(jnp.int32, (SLOTS, ROWS), 0).astype(F32)
    within = slot_f - MOST * jnp.floor((slot_f + 0.5) * (1.0 / MOST))
    named_at = dot(spread, named)
    rank_at = dot(spread, rank.astype(BF16))
    chosen = jnp.where((named_at > 0.5) & (jnp.abs(rank_at - within) < 0.5), 1.0, 0.0)
    gather = chosen.astype(BF16)

    def pick_rows(source, start, width):
        at = pl.ds(pl.multiple_of(start, 128), width)
        return dot(gather, source[:, at]).reshape(EP, MOST, width).astype(BF16)

    send_h[...] = pick_rows(hid, tp * RING, RING)

    def make_picks():
        weight = first * weights[0:1, :] + second * weights[1:2, :]
        weight_hi = weight.astype(BF16)
        weight_lo = (weight - weight_hi.astype(F32)).astype(BF16)
        picks[0:ROWS, :] = jnp.transpose(chosen * dot(spread, weight_hi)).astype(BF16)
        picks[ROWS:, :] = jnp.transpose(chosen * dot(spread, weight_lo)).astype(BF16)

    def remote(src, dst, send, recv, device):
        return pltpu.make_async_remote_copy(
            src_ref=src, dst_ref=dst, send_sem=send, recv_sem=recv, device_id=device, device_id_type=MESH
        )

    def arrived(view, sem):
        remote(view, view, sem, sem, (pod, me, right)).wait_recv()

    def sent(view, sem):
        remote(view, view, sem, sem, (pod, me, right)).wait_send()

    def dispatch(a, send, rows, recv):
        for dz, dx in STEPS:
            peer = expert_at(dz, dx)
            remote(send.at[peer], rows.at[me], disp_s.at[a], recv(dz), (pod, peer, tp)).start()
        pltpu.make_async_copy(send.at[me], rows.at[me], recv(0)).start()

    first_cols, first_cols_g = pl.ds(0, DIRECT), pl.ds(0, DIRECT_G)
    piece_o[:, :, first_cols] = pick_rows(hid, TP * RING, DIRECT)
    pl.semaphore_wait(barrier, len(STEPS) + 4)
    dispatch(0, send_h, rows_h.at[tp], lambda dz: disp_r.at[0, dz])
    for i in range(3):
        remote(
            dense_hbm.at[i], dense_w.at[i, own_rows], core_s.at[i], core_r.at[i], (1 - pod, me, tp)
        ).start()
    dispatch(2, piece_o.at[:, :, first_cols], rows_d, lambda dz: direct_r.at[0])
    row_loads[1].wait()
    send_g[...] = pick_rows(grad, tp * RING_G, RING_G)
    dispatch(1, send_g, rows_g.at[tp], lambda dz: disp_r.at[1, dz])
    if DIRECT_G:
        piece_g[:, :, first_cols_g] = pick_rows(grad, TP * RING_G, DIRECT_G)
        dispatch(3, piece_g.at[:, :, first_cols_g], rows_e, lambda dz: direct_r.at[1])

    def group_of(rows, q, dz):
        at = pl.multiple_of(lax.rem(z - dz + 4, 4) * 4, 4)
        return rows.at[q, pl.ds(at, 4)]

    def ring_out(a, rows, some=(0, 1, 2, 3)):
        for n in some:
            block = group_of(rows, tp, GROUPS[n])
            arrived(block, disp_r.at[a, GROUPS[n]])
            for way, peer in ((0, right), (1, left)):
                remote(block, block, ring_s.at[a], ring_r.at[a, way, n], (pod, me, peer)).start()

    def ring_on(a, rows, way):
        source, peer = ((left, right), (right, left))[way]
        for n in (2 * way, 2 * way + 1):
            block = group_of(rows, source, GROUPS[n])
            arrived(block, ring_r.at[a, way, n])
            remote(block, block, fwd_s.at[a], fwd_r.at[a], (pod, me, peer)).start()

    def ring_in(a, rows, way):
        source = (left, right)[way]
        for n in (2 - 2 * way, 3 - 2 * way):
            arrived(group_of(rows, source, GROUPS[n]), ring_r.at[a, way, n])

    def ring_end(a, rows):
        arrived(rows.at[lax.rem(tp + 2, TP)], fwd_r.at[a])

    def pack(rows, width):
        def step(i, carry):
            block = rows[pl.ds(2 * i, 2)]
            mat_x[pl.ds(pl.multiple_of(i * 2 * MOST, 16), 2 * MOST), 0:width] = (
                block.astype(F32).reshape(2 * MOST, width).astype(BF16)
            )
            return carry

        lax.fori_loop(0, EP // 2, step, 0)

    def forward_part(rows, at, width, start):
        pack(rows, width)
        if start:
            acc_gate[...] = dot(mat_x[:, 0:width], gate_up[0, at, :])
            acc_up[...] = dot(mat_x[:, 0:width], gate_up[1, at, :])
        else:
            acc_gate[...] += dot(mat_x[:, 0:width], gate_up[0, at, :])
            acc_up[...] += dot(mat_x[:, 0:width], gate_up[1, at, :])

    def forward_quarter(q, start):
        at = pl.ds(pl.multiple_of(q * RING, RING), RING)
        forward_part(rows_h.at[q], at, RING, start)

    def backward_part(rows, at, width, start):
        pack(rows, width)
        if start:
            acc_grad[...] = dot(mat_x[:, 0:width], down[at, :])
        else:
            acc_grad[...] += dot(mat_x[:, 0:width], down[at, :])

    def backward_quarter(q, start):
        at = pl.ds(pl.multiple_of(q * RING_G, RING_G), RING_G)
        backward_part(rows_g.at[q], at, RING_G, start)

    def dense_in(i, which):
        at = (own_rows, other_rows)[which]
        left_side = (hid, hid, grad)[i]
        if which == 0:
            dense_loads[i].wait()
            dense_acc[i] = dot(left_side[:, at], dense_w[i, at, :])
        else:
            dense_acc[i] += dot(left_side[:, at], dense_w[i, at, :])

    def dense_landed(i):
        landed = dense_w.at[i, other_rows]
        remote(dense_hbm.at[i], landed, core_s.at[i], core_r.at[i], (1 - pod, me, tp)).wait_recv()

    for i in range(3):
        dense_in(i, 0)
    ring_out(0, rows_h)
    for load in loads:
        load.wait()
    forward_quarter(tp, True)
    dense_landed(0)
    dense_in(0, 1)
    ring_on(0, rows_h, 0)
    dense_landed(1)
    dense_in(1, 1)
    ring_on(0, rows_h, 1)
    ring_in(0, rows_h, 0)
    forward_quarter(left, False)
    ring_in(0, rows_h, 1)
    forward_quarter(right, False)
    arrived(rows_d, direct_r.at[0])
    forward_part(rows_d, pl.ds(TP * RING, DIRECT), DIRECT, False)
    ring_out(1, rows_g, (0, 1))
    ring_end(0, rows_h)
    forward_quarter(lax.rem(tp + 2, TP), False)
    ring_out(1, rows_g, (2, 3))
    peers = pl.ds(0, len(STEPS))
    sent(piece_o.at[peers, :, first_cols], disp_s.at[2])

    silu, slope = silu_parts(acc_gate[...])
    act[0] = (silu * acc_up[...]).astype(BF16)

    def block_at(q):
        return pl.ds(pl.multiple_of(WHOLE_G + q * BLOCK, BLOCK), BLOCK)

    def span(a, c):
        return pl.ds(*((PARTS_O, PARTS_G)[a][c]))

    def send_back(a, c, piece, back):
        cols = span(a, c)
        for dz, dx in STEPS:
            peer = expert_at(dz, dx)
            remote(
                piece.at[peer, :, cols], back.at[me, :, cols], ret_s.at[a, c], ret_r.at[a, c], (pod, peer, tp)
            ).start()
        pltpu.make_async_copy(piece.at[me, :, cols], back.at[me, :, cols], ret_r.at[a, c]).start()

    for c in range(4):
        cols = span(0, c)
        piece_o[:, :, cols] = dot_t(act[0], down[cols, :]).reshape(EP, MOST, cols.size).astype(BF16)
        send_back(0, c, piece_o, back_o)

    dense_landed(2)
    dense_in(2, 1)
    ring_on(1, rows_g, 0)
    d_silu, d_slope = silu_parts(dense_acc[0])
    d_up, d_back = dense_acc[1], dense_acc[2]
    d_act = (d_silu * d_up).astype(BF16)
    d_grad_gate = (d_back * d_up * d_slope).astype(BF16)
    d_grad_up = (d_back * d_silu).astype(BF16)
    for c in range(2):
        half = pl.ds(c * HALF, HALF)
        dense_out[:, half] = dot_t(d_act, dense_w[2, half, :]).astype(BF16)
    ring_on(1, rows_g, 1)
    for c in range(2):
        half = pl.ds(c * HALF, HALF)
        total = dot_t(d_grad_gate, dense_w[0, half, :]) + dot_t(d_grad_up, dense_w[1, half, :])
        dense_grad[:, half] = total.astype(BF16)
    make_picks()
    for d in (2, 1, 3):
        peer = lax.rem(tp + d, TP)
        remote(
            dense_grad.at[:, block_at(peer)], dense_in_x.at[d - 1], dense_s.at[0], dense_r.at[0], (pod, me, peer)
        ).start()
    mine = pl.ds(pl.multiple_of(tp * OWN, OWN), OWN)

    def combine(a, c, back, dense, part, red):
        cols = span(a, c)
        arrived(back.at[:, :, cols], ret_r.at[a, c])
        rows = back[:, :, cols].astype(F32).reshape(SLOTS, cols.size).astype(BF16)
        product = dot(picks[...], rows)
        total = dense[:, cols].astype(F32) + product[:ROWS] + product[ROWS:]
        part[:, cols] = total.astype(BF16)
        for d in (2, 1, 3):
            peer = lax.rem(tp + d, TP)
            rows_at = pl.ds(pl.multiple_of(peer * OWN, OWN), OWN)
            remote(
                part.at[rows_at, cols], red.at[d - 1, :, cols], red_s.at[a, c], red_r.at[a, c], (pod, me, peer)
            ).start()

    def reduced(a, c, part, red):
        cols = span(a, c)
        total = part[mine, cols].astype(F32)
        arrived(red.at[:, :, cols], red_r.at[a, c])
        for d in range(3):
            total = total + red[d, :, cols].astype(F32)
        return total

    def spread_out(k, ref, target):
        for d in (2, 1, 3):
            remote(ref, target, gat_s.at[k], gat_r.at[k], (pod, me, lax.rem(tp + d, TP))).start()
        pltpu.make_async_copy(ref, target, gat_r.at[k]).start()

    others = pl.ds(0, ROWS - OWN)

    def combine_o(c):
        combine(0, c, back_o, dense_out, part_o, red_o)

    def reduce_o(c):
        cols = span(0, c)
        total = reduced(0, c, part_o, red_o)
        part_o[mine, cols] = (tok[mine, cols].astype(F32) + total).astype(BF16)
        spread_out(c, part_o.at[mine, cols], layer_out.at[mine, cols])

    backward_quarter(tp, True)
    ring_in(1, rows_g, 0)
    backward_quarter(left, False)
    ring_in(1, rows_g, 1)
    backward_quarter(right, False)
    if DIRECT_G:
        arrived(rows_e, direct_r.at[1])
        backward_part(rows_e, pl.ds(TP * RING_G, DIRECT_G), DIRECT_G, False)
    combine_o(0)
    ring_end(1, rows_g)
    backward_quarter(lax.rem(tp + 2, TP), False)
    if DIRECT_G:
        sent(piece_g.at[peers, :, first_cols_g], disp_s.at[3])
    silu, slope = silu_parts(acc_gate[...])
    act[0] = (acc_grad[...] * acc_up[...] * slope).astype(BF16)
    act[1] = (acc_grad[...] * silu).astype(BF16)

    def grad_piece(cols):
        return dot_t(act[0], gate_up[0, cols, :]) + dot_t(act[1], gate_up[1, cols, :])

    for d in (2, 1, 3):
        peer = lax.rem(tp + d, TP)
        cross_out[d - 1] = grad_piece(block_at(peer)).reshape(EP, MOST, BLOCK).astype(BF16)
        remote(
            cross_out.at[d - 1], cross_in.at[d - 1], cross_s.at[0], cross_r.at[0], (pod, me, peer)
        ).start()
    for c in range(len(PARTS_G)):
        cols = span(1, c)
        piece_g[:, :, cols] = grad_piece(cols).reshape(EP, MOST, cols.size).astype(BF16)
        send_back(1, c, piece_g, back_g)
        if c == 0:
            combine_o(1)
            reduce_o(0)
    merged[...] = grad_piece(block_at(tp)).reshape(EP, MOST, BLOCK).astype(BF16)

    def merge():
        total = merged[...].astype(F32)
        arrived(cross_in, cross_r.at[0])
        for d in range(3):
            total = total + cross_in[d].astype(F32)
        merged[...] = total.astype(BF16)
        for dz, dx in STEPS:
            peer = expert_at(dz, dx)
            remote(merged.at[peer], back_x.at[me], retx_s.at[0], retx_r.at[0], (pod, peer, tp)).start()
        pltpu.make_async_copy(merged.at[me], back_x.at[me], retx_r.at[0]).start()

    def combine_x():
        arrived(back_x, retx_r.at[0])
        rows = back_x[...].astype(F32).reshape(SLOTS, BLOCK).astype(BF16)
        product = dot(picks[...], rows)
        total = dense_grad[:, block_at(tp)].astype(F32) + product[:ROWS] + product[ROWS:]
        arrived(dense_in_x, dense_r.at[0])
        for d in range(3):
            total = total + dense_in_x[d].astype(F32)
        dense_in_x[0] = total.astype(BF16)
        spread_out(2 * PARTS - 1, dense_in_x.at[0], total_g.at[:, block_at(tp)])

    def combine_g(c):
        combine(1, c, back_g, dense_grad, part_g, red_g)

    def reduce_g(c):
        cols = span(1, c)
        part_g[mine, cols] = reduced(1, c, part_g, red_g).astype(BF16)
        spread_out(PARTS + c, part_g.at[mine, cols], total_g.at[mine, cols])

    combine_o(2)
    reduce_o(1)
    merge()
    combine_o(3)
    reduce_o(2)
    reduce_o(3)
    combine_g(0)
    for c in range(1, len(PARTS_G)):
        combine_g(c)
        reduce_g(c - 1)
    combine_x()
    reduce_g(len(PARTS_G) - 1)

    for c in range(4):
        arrived(layer_out.at[:, span(0, c)], gat_r.at[c])
        sent(part_o.at[others, span(0, c)], gat_s.at[c])
        sent(red_o.at[:, :, span(0, c)], red_s.at[0, c])
        sent(piece_o.at[peers, :, span(0, c)], ret_s.at[0, c])
    for c in range(len(PARTS_G)):
        arrived(total_g.at[:, span(1, c)], gat_r.at[PARTS + c])
        sent(part_g.at[others, span(1, c)], gat_s.at[PARTS + c])
        sent(red_g.at[:, :, span(1, c)], red_s.at[1, c])
        sent(piece_g.at[peers, :, span(1, c)], ret_s.at[1, c])
    arrived(total_g.at[:, pl.ds(WHOLE_G, TP * BLOCK)], gat_r.at[2 * PARTS - 1])
    sent(dense_in_x, gat_s.at[2 * PARTS - 1])
    sent(dense_in_x, dense_s.at[0])
    sent(cross_out, cross_s.at[0])
    sent(merged.at[peers], retx_s.at[0])
    for i in range(3):
        sent(dense_hbm.at[i], core_s.at[i])
    for a, send, rows in ((0, send_h, rows_h), (1, send_g, rows_g)):
        sent(send.at[peers], disp_s.at[a])
        sent(rows.at[pl.ds(0, 2)], ring_s.at[a])
        sent(rows.at[0], fwd_s.at[a])


def finish(tok, gain, grad, total_g, layer_in, layer_out, grad_in):
    layer_out[...] = layer_in[...]
    float_in = tok[...].astype(F32)
    inverse = lax.rsqrt(jnp.mean(float_in * float_in, axis=1, keepdims=True) + EPS)
    normed = float_in * inverse
    scaled = total_g[...].astype(F32) * gain[...].reshape(1, D)
    project = jnp.mean(scaled * normed, axis=1, keepdims=True)
    grad_in[...] = (grad[...].astype(F32) + inverse * (scaled - normed * project)).astype(BF16)


def body(tokens, norm_gain, dense_weight, expert_gate_up, expert_down, expert_ids, gate_weights, grad_out):
    vmem = pl.BlockSpec(memory_space=pltpu.VMEM)
    hbm = pl.BlockSpec(memory_space=pl.ANY)
    dma = pltpu.SemaphoreType.DMA
    steps = len(STEPS)
    row_shape = jax.ShapeDtypeStruct((ROWS, D), BF16)
    layer_sum, grad_sum = pl.pallas_call(
        kernel,
        name="layer",
        out_shape=[row_shape, row_shape],
        in_specs=[hbm, vmem, hbm, hbm, hbm, vmem, vmem, hbm],
        out_specs=[hbm, hbm],
        scratch_shapes=[
            pltpu.VMEM((ROWS, D), BF16),
            pltpu.VMEM((ROWS, D), BF16),
            pltpu.VMEM((3, D, FF), BF16),
            pltpu.VMEM((2, D, FF), BF16),
            pltpu.VMEM((D, FF), BF16),
            pltpu.VMEM((ROWS, D), BF16),
            pltpu.VMEM((EP, MOST, RING), BF16),
            pltpu.VMEM((EP, MOST, RING_G), BF16),
            pltpu.VMEM((TP, EP, MOST, RING), BF16),
            pltpu.VMEM((EP, MOST, DIRECT), BF16),
            pltpu.VMEM((TP, EP, MOST, RING_G), BF16),
            pltpu.VMEM((EP, MOST, max(DIRECT_G, 128)), BF16),
            pltpu.VMEM((SLOTS, max(DIRECT, RING_G)), BF16),
            pltpu.VMEM((SLOTS, FF), F32),
            pltpu.VMEM((SLOTS, FF), F32),
            pltpu.VMEM((SLOTS, FF), F32),
            pltpu.VMEM((2, SLOTS, FF), BF16),
            pltpu.VMEM((ROWS, D), BF16),
            pltpu.VMEM((ROWS, D), BF16),
            pltpu.VMEM((EP, MOST, D), BF16),
            pltpu.VMEM((EP, MOST, WHOLE_G), BF16),
            pltpu.VMEM((EP, MOST, D), BF16),
            pltpu.VMEM((EP, MOST, WHOLE_G), BF16),
            pltpu.VMEM((ROWS, D), BF16),
            pltpu.VMEM((ROWS, WHOLE_G), BF16),
            pltpu.VMEM((3, OWN, D), BF16),
            pltpu.VMEM((3, OWN, WHOLE_G), BF16),
            pltpu.VMEM((2 * ROWS, SLOTS), BF16),
            pltpu.VMEM((3, ROWS, FF), F32),
            pltpu.VMEM((3, EP, MOST, BLOCK), BF16),
            pltpu.VMEM((3, EP, MOST, BLOCK), BF16),
            pltpu.VMEM((EP, MOST, BLOCK), BF16),
            pltpu.VMEM((EP, MOST, BLOCK), BF16),
            pltpu.VMEM((3, ROWS, BLOCK), BF16),
            dma((7,)),
            dma((3,)),
            dma((3,)),
            dma((4,)),
            dma((2,)),
            dma((2, 2, 4)),
            dma((2,)),
            dma((2,)),
            dma((2, 4)),
            dma((2,)),
            dma((2, PARTS)),
            dma((2, PARTS)),
            dma((2, PARTS)),
            dma((2, PARTS)),
            dma((2 * PARTS,)),
            dma((2 * PARTS,)),
            dma((1,)),
            dma((1,)),
            dma((1,)),
            dma((1,)),
            dma((1,)),
            dma((1,)),
        ],
        compiler_params=pltpu.CompilerParams(
            collective_id=0, has_side_effects=True, vmem_limit_bytes=63 * 2**20
        ),
    )(
        tokens, norm_gain, dense_weight, expert_gate_up, expert_down,
        expert_ids.T, gate_weights.T, grad_out,
    )
    block = pl.BlockSpec((ROWS // 2, D), lambda i: (i, 0))
    return pl.pallas_call(
        finish,
        name="finish",
        grid=(2,),
        out_shape=[row_shape, row_shape],
        in_specs=[block, pl.BlockSpec((D,), lambda i: (0,)), block, block, block],
        out_specs=[block, block],
    )(tokens, norm_gain, grad_out, grad_sum, layer_sum)


def solution(mesh):
    rows = P(("outer", "ep"), None)
    in_specs = (rows, P(), P(None, "outer", "tp"), P("ep", None, None, "tp"), P("ep", None, "tp"), rows, rows, rows)
    return jax.shard_map(body, mesh=mesh, in_specs=in_specs, out_specs=(rows, rows), check_vma=False)
```
